512 devices in a mesh: ctx: 64 (over z, y), tp: 8 (over x, core).
Axes of the slice: x: 4, y: 4, z: 16, core: 2. Of those that a mesh axis runs over, the one named last changes fastest.
Arguments:
- queries: bfloat16 [16384, 32, 128], P('ctx', 'tp'), may hold values from -6 to 6
- keys: bfloat16 [16384, 32, 128], P('ctx', 'tp'), may hold values from -6 to 6
- values: bfloat16 [16384, 32, 128], P('ctx', 'tp'), may hold values from -6 to 6
- init_state: float32 [32, 128, 128], P('tp'), may hold values from -192 to 192
- gain: float32 [32, 128], P('tp'), may hold values from 0.1 to 1.9
- cotangent: bfloat16 [16384, 32, 128], P('ctx', 'tp'), may hold values from -6 to 6
Outputs:
- normed: bfloat16 [16384, 32, 128], P('ctx', 'tp')
- d_query: bfloat16 [16384, 32, 128], P('ctx', 'tp')
- d_key: bfloat16 [16384, 32, 128], P('ctx', 'tp')
- d_value: bfloat16 [16384, 32, 128], P('ctx', 'tp')
- d_state: float32 [32, 128, 128], P('tp')
- d_gain: float32 [32, 128], P('tp')
The draws below stay inside these ranges and needn't reach their ends.
All inputs are finite; a program needn't handle non-finite values.
Results may differ from the reference program's by a relative error of at most 0.005.
Values sent between devices are 32-bit elements; how exact they have to be, the bound alone decides.
No kernel may reach another device: no remote copies, remote signals or barrier semaphores. Data moves between devices by JAX's collectives and lax.ppermute only.
A program may use at most 64 MiB of HBM per device.

```python
import jax
import jax.numpy as jnp
from jax import lax

DH = 128
H = 32
BLK = 256
TOKENS = 16384


def steps_of(own_key, shape, cuts, low, top_value):
    def one(dim, blocks):
        draws = jax.random.uniform(jax.random.fold_in(jax.random.fold_in(own_key, 6), dim), (blocks,), jnp.float32, low / len(cuts), top_value / len(cuts))
        return jnp.repeat(jnp.exp(draws), shape[dim] // blocks).reshape((-1,) + (1,) * (len(shape) - dim - 1))

    level = one(*cuts[0])
    for cut in cuts[1:]:
        level = level * one(*cut)
    return level


def centred(stream_key, shape, scale, reach, pieces=(), dtype=jnp.bfloat16):
    values = scale * jax.random.normal(stream_key, shape, jnp.float32)
    if pieces:
        values = values * steps_of(stream_key, shape, pieces, -0.22, 0.18)
    return jnp.clip(values, -reach, reach).astype(dtype)


def setup_inputs(seed: int = 0) -> dict:
    streams_of = jax.random.split(jax.random.key(seed), 7)
    queries = centred(streams_of[0], (TOKENS, H, DH), 1.0, 6.0, ((0, 64), (1, 8)))
    keys = centred(streams_of[1], (TOKENS, H, DH), 1.0, 6.0, ((0, 64), (1, 8)))
    values = centred(streams_of[2], (TOKENS, H, DH), 1.0, 6.0, ((0, 64), (1, 8)))
    init_state = centred(streams_of[3], (H, DH, DH), 32.0, 192.0, ((0, 8),), jnp.float32)
    gain = jnp.clip(1.0 + 0.18 * jax.random.normal(streams_of[4], (H, DH), jnp.float32), 0.1, 1.9)
    cotangent = centred(streams_of[5], (TOKENS, H, DH), 1.0, 6.0, ((0, 64), (1, 8)))
    return {"queries": queries, "keys": keys, "values": values, "init_state": init_state, "gain": gain, "cotangent": cotangent}


HIGH = lax.Precision.HIGHEST

def reference(queries, keys, values, init_state, gain, cotangent):
    blocks = TOKENS // BLK
    query_b = queries.astype(jnp.float32).reshape(blocks, BLK, H, DH)
    key_b = keys.astype(jnp.float32).reshape(blocks, BLK, H, DH)
    value_b = values.astype(jnp.float32).reshape(blocks, BLK, H, DH)
    cot_b = cotangent.astype(jnp.float32).reshape(blocks, BLK, H, DH)
    rows = jnp.arange(BLK)
    causal = rows[:, None] >= rows[None, :]
    block_state = jnp.einsum('bjhd,bjhe->bhde', key_b, value_b, precision=HIGH)
    zero_one = jnp.zeros((1, H, DH, DH), jnp.float32)
    earlier = jnp.concatenate([zero_one, jnp.cumsum(block_state[:-1], axis=0)], axis=0)
    state_before = init_state[None] + earlier

    def forward(item):
        qb, kb, vb, sb = item
        scores = jnp.einsum('ihd,jhd->hij', qb, kb, precision=HIGH)
        scores = jnp.where(causal[None], scores, 0.0).astype(jnp.bfloat16)
        attn = jnp.einsum('hij,jhe->ihe', scores.astype(jnp.float32), vb, precision=HIGH)
        return attn + jnp.einsum('ihd,hde->ihe', qb, sb, precision=HIGH)
    attn = lax.map(forward, (query_b, key_b, value_b, state_before))
    width_total = H * DH
    ssq = lax.optimization_barrier(jnp.sum(attn * attn, axis=(2, 3)))
    rscale = lax.rsqrt(ssq / width_total + 1e-06)[:, :, None, None]
    normed = (attn * rscale * gain).astype(jnp.bfloat16).reshape(TOKENS, H, DH)
    gdot = lax.optimization_barrier(jnp.sum(gain * cot_b * attn, axis=(2, 3)))[:, :, None, None]
    d_attn = (rscale * gain * cot_b - attn * rscale ** 3 * gdot / width_total).astype(jnp.bfloat16)
    d_attn32 = d_attn.astype(jnp.float32)
    d_gain = lax.optimization_barrier(jnp.sum(cot_b * attn * rscale, axis=(0, 1)))
    grad_block = jnp.einsum('bihd,bihe->bhde', query_b, d_attn32, precision=HIGH)
    later_part = jnp.flip(jnp.cumsum(jnp.flip(grad_block[1:], 0), axis=0), 0)
    grad_after = jnp.concatenate([later_part, zero_one], axis=0)
    d_state = lax.optimization_barrier(jnp.sum(grad_block, axis=0))

    def backward(item):
        qb, kb, vb, db, sb, gb = item
        scores = jnp.einsum('ihd,jhd->hij', qb, kb, precision=HIGH)
        scores = jnp.where(causal[None], scores, 0.0).astype(jnp.bfloat16).astype(jnp.float32)
        back = jnp.einsum('ihe,jhe->hij', db, vb, precision=HIGH)
        back = jnp.where(causal[None], back, 0.0).astype(jnp.bfloat16).astype(jnp.float32)
        dq = jnp.einsum('hij,jhd->ihd', back, kb, precision=HIGH) + jnp.einsum('ihe,hde->ihd', db, sb, precision=HIGH)
        dk = jnp.einsum('hij,ihd->jhd', back, qb, precision=HIGH) + jnp.einsum('jhe,hde->jhd', vb, gb, precision=HIGH)
        dv = jnp.einsum('hij,ihe->jhe', scores, db, precision=HIGH) + jnp.einsum('jhd,hde->jhe', kb, gb, precision=HIGH)
        return (dq.astype(jnp.bfloat16), dk.astype(jnp.bfloat16), dv.astype(jnp.bfloat16))
    d_query, d_key, d_value = lax.map(backward, (query_b, key_b, value_b, d_attn32, state_before, grad_after))
    return (normed, d_query.reshape(TOKENS, H, DH), d_key.reshape(TOKENS, H, DH), d_value.reshape(TOKENS, H, DH), d_state, d_gain)
```

```python
import functools

import jax
import jax.numpy as jnp
from jax import lax
from jax.experimental import pallas as pl
from jax.experimental.pallas import tpu as pltpu
from jax.sharding import PartitionSpec as P

F32 = jnp.float32
BF16 = jnp.bfloat16
EPS = 1e-06
NN = (((1,), (0,)), ((), ()))
NT = (((1,), (1,)), ((), ()))
TN = (((0,), (0,)), ((), ()))


def dot(a, b, dims):
    return lax.dot_general(a, b, dims, preferred_element_type=F32)


def split(a):
    high = a.astype(BF16)
    return high, (a - high.astype(F32)).astype(BF16)


def times(a, m, turned):
    high, low = split(m)
    both = jnp.concatenate([high, low], axis=1 if turned else 0)
    return dot(jnp.concatenate([a, a], axis=1), both, NT if turned else NN)


def head_rows(h, tokens, heads):
    return pl.ds(h, tokens, stride=heads)


def causal(tokens):
    rows = lax.broadcasted_iota(jnp.int32, (tokens, tokens), 0)
    cols = lax.broadcasted_iota(jnp.int32, (tokens, tokens), 1)
    return rows >= cols


def state_kernel(k_ref, v_ref, state_ref, kh_ref, vh_ref, k32, v32):
    heads, tokens, _ = kh_ref.shape
    k32[...] = k_ref[...].astype(F32)
    v32[...] = v_ref[...].astype(F32)
    for h in range(heads):
        k = k32[head_rows(h, tokens, heads), :].astype(BF16)
        v = v32[head_rows(h, tokens, heads), :].astype(BF16)
        state_ref[h] = dot(k, v, TN)
        kh_ref[h] = k
        vh_ref[h] = v


def local_kernel(q_ref, kh_ref, vh_ref, qh_ref, scores_ref, attn_ref, q32):
    heads, tokens, _ = kh_ref.shape
    q32[...] = q_ref[...].astype(F32)
    keep = causal(tokens)
    for h in range(heads):
        q = q32[head_rows(h, tokens, heads), :].astype(BF16)
        qh_ref[h] = q
        scores = jnp.where(keep, dot(q, kh_ref[h], NT), 0.0).astype(BF16)
        scores_ref[h] = scores
        attn_ref[h] = dot(scores, vh_ref[h], NN)


def cot_kernel(c_ref, gain_ref, ch_ref, c32):
    heads, tokens, _ = ch_ref.shape
    c32[...] = c_ref[...].astype(F32)
    for h in range(heads):
        ch_ref[h] = c32[head_rows(h, tokens, heads), :]


def prefix_kernel(x_ref, out_ref):
    peers = x_ref.shape[0]
    total = jnp.zeros(x_ref.shape[1:], F32)
    for i in range(peers):
        out_ref[i] = total
        total = total + x_ref[i]


def suffix_kernel(x_ref, out_ref):
    peers, rows = x_ref.shape[:2]
    total = jnp.zeros(x_ref.shape[1:], F32)
    for i in reversed(range(peers)):
        out_ref[i, :rows] = total
        total = total + x_ref[i]
    for i in range(peers):
        out_ref[i, rows:] = total


def attn_kernel(before_ref, init_ref, qh_ref, local_ref, ch_ref, gain_ref, attn_ref, state_ref, stats_ref):
    heads, tokens, width = qh_ref.shape
    ssq = jnp.zeros((tokens, width), F32)
    gdot = jnp.zeros((tokens, width), F32)
    for h in range(heads):
        state = init_ref[h] + before_ref[h]
        state_ref[h] = state
        attn = local_ref[h] + times(qh_ref[h], state, False)
        attn_ref[h] = attn
        ssq = ssq + attn * attn
        gdot = gdot + gain_ref[h : h + 1, :] * ch_ref[h] * attn
    ssq_row = jnp.sum(ssq.T, axis=0, keepdims=True)
    gdot_row = jnp.sum(gdot.T, axis=0, keepdims=True)
    half = tokens // 2
    rows = jnp.concatenate(
        [ssq_row[:, :half], ssq_row[:, half:], gdot_row[:, :half], gdot_row[:, half:]], axis=0
    )
    for i in range(stats_ref.shape[0]):
        stats_ref[i] = rows


def grad_kernel(width_total, stats_ref, attn_ref, ch_ref, gain_ref, qh_ref, dh_ref, grad_ref, scale_ref):
    heads, tokens, width = qh_ref.shape
    rows = stats_ref[0]
    for i in range(1, stats_ref.shape[0]):
        rows = rows + stats_ref[i]
    ssq = jnp.concatenate([rows[0:1], rows[1:2]], axis=1)
    gdot = jnp.concatenate([rows[2:3], rows[3:4]], axis=1)
    rscale = lax.rsqrt(ssq / width_total + EPS)
    pull = rscale * rscale * rscale * gdot / width_total
    rscale = jnp.broadcast_to(rscale, (width, tokens)).T
    pull = jnp.broadcast_to(pull, (width, tokens)).T
    scale_ref[...] = rscale
    for h in range(heads):
        gain = gain_ref[h : h + 1, :]
        d_attn = (rscale * gain * ch_ref[h] - attn_ref[h] * pull).astype(BF16)
        dh_ref[h] = d_attn
        grad_ref[h] = dot(qh_ref[h], d_attn, TN)


def gain_kernel(attn_ref, ch_ref, gain_ref, scale_ref, normed_ref, term_ref, out32):
    heads, tokens, _ = ch_ref.shape
    rscale = scale_ref[...]
    terms = []
    for h in range(heads):
        scaled = attn_ref[h] * rscale
        out32[head_rows(h, tokens, heads), :] = scaled * gain_ref[h : h + 1, :]
        terms.append(jnp.sum(ch_ref[h] * scaled, axis=0, keepdims=True))
    normed_ref[...] = out32[...].astype(BF16)
    term = jnp.concatenate(terms, axis=0)
    for i in range(term_ref.shape[0]):
        term_ref[i] = term


def back_kernel(dh_ref, vh_ref, kh_ref, qh_ref, state_ref, scores_ref, dq_ref, dk_ref, dv_ref, out32):
    heads, tokens, _ = kh_ref.shape
    keep = causal(tokens)
    for h in range(heads):
        d_attn = dh_ref[h]
        back = jnp.where(keep, dot(d_attn, vh_ref[h], NT), 0.0).astype(BF16)
        d_query = dot(back, kh_ref[h], NN) + times(d_attn, state_ref[h], True)
        out32[head_rows(h, tokens, heads), :] = d_query
        dk_ref[h] = dot(back, qh_ref[h], TN)
        dv_ref[h] = dot(scores_ref[h], d_attn, TN)
    dq_ref[...] = out32[...].astype(BF16)


def last_kernel(after_ref, kh_ref, vh_ref, dk_in, dv_in, dk_ref, dv_ref, k32, v32):
    heads, tokens, _ = kh_ref.shape
    for h in range(heads):
        after = after_ref[h]
        k32[head_rows(h, tokens, heads), :] = dk_in[h] + times(vh_ref[h], after, True)
        v32[head_rows(h, tokens, heads), :] = dv_in[h] + times(kh_ref[h], after, False)
    dk_ref[...] = k32[...].astype(BF16)
    dv_ref[...] = v32[...].astype(BF16)


def sum_kernel(x_ref, out_ref):
    total = x_ref[0]
    for i in range(1, x_ref.shape[0]):
        total = total + x_ref[i]
    out_ref[...] = total


def call(kernel, name, outs, args, scratch=(), flops=0):
    moved = sum(a.size * a.dtype.itemsize for a in list(args) + list(outs))
    return pl.pallas_call(
        kernel,
        name=name,
        out_shape=outs,
        in_specs=[pl.BlockSpec(memory_space=pltpu.VMEM)] * len(args),
        out_specs=[pl.BlockSpec(memory_space=pltpu.VMEM)] * len(outs),
        scratch_shapes=scratch,
        compiler_params=pltpu.CompilerParams(vmem_limit_bytes=24 * 2**20),
        cost_estimate=pl.CostEstimate(flops=flops, bytes_accessed=moved, transcendentals=0),
    )(*args)


def shape(dims, dtype=F32):
    return jax.ShapeDtypeStruct(dims, dtype)


def on_device(queries, keys, values, init_state, gain, cotangent):
    tokens, heads, width = queries.shape
    peers = lax.axis_size("ctx")
    sharers = lax.axis_size("tp")
    width_total = heads * sharers * width
    flat = (tokens * heads, width)
    by_head = (heads, tokens, width)
    states = (heads, width, width)
    chunk = heads * width // peers
    chunks = (peers, chunk, width)
    squares = (heads, tokens, tokens)
    wide = pltpu.VMEM(flat, F32)
    unit = 2 * tokens * width * width * heads
    q, k, v, c = (a.reshape(flat) for a in (queries, keys, values, cotangent))

    own, kh, vh = call(
        state_kernel,
        "state",
        [shape(states), shape(by_head, BF16), shape(by_head, BF16)],
        [k, v],
        [wide, wide],
        unit,
    )
    gathered = lax.all_to_all(own.reshape(chunks), "ctx", 0, 0)
    qh, scores, local = call(
        local_kernel,
        "local",
        [shape(by_head, BF16), shape(squares, BF16), shape(by_head)],
        [q, kh, vh],
        [wide],
        4 * unit,
    )
    (before,) = call(prefix_kernel, "prefix", [shape(chunks)], [gathered])
    c, before = lax.optimization_barrier((c, before))
    before = lax.all_to_all(before, "ctx", 0, 0).reshape(states)
    (ch,) = call(cot_kernel, "cotangent", [shape(by_head)], [c, gain], [wide])
    attn, state, stats = call(
        attn_kernel,
        "attn",
        [shape(by_head), shape(states), shape((sharers, 4, tokens // 2))],
        [before, init_state, qh, local, ch, gain],
        (),
        2 * unit,
    )
    stats = lax.all_to_all(stats, "tp", 0, 0)
    dh, grad, scale = call(
        functools.partial(grad_kernel, width_total),
        "grad",
        [shape(by_head, BF16), shape(states), shape((tokens, width))],
        [stats, attn, ch, gain, qh],
        (),
        unit,
    )
    gathered = lax.all_to_all(grad.reshape(chunks), "ctx", 0, 0)
    normed, term = call(
        gain_kernel,
        "normed",
        [shape(flat, BF16), shape((peers, heads, width))],
        [attn, ch, gain, scale],
        [wide],
    )
    term = lax.all_to_all(term, "ctx", 0, 0)
    (after,) = call(suffix_kernel, "suffix", [shape((peers, 2 * chunk, width))], [gathered])
    dh, after = lax.optimization_barrier((dh, after))
    after = lax.all_to_all(after, "ctx", 0, 0)
    d_query, dk, dv = call(
        back_kernel,
        "back",
        [shape(flat, BF16), shape(by_head), shape(by_head)],
        [dh, vh, kh, qh, state, scores],
        [wide],
        10 * unit,
    )
    d_state = after[:, chunk:].reshape(states)
    after = after[:, :chunk].reshape(states)
    d_key, d_value = call(
        last_kernel,
        "last",
        [shape(flat, BF16), shape(flat, BF16)],
        [after, kh, vh, dk, dv],
        [wide, wide],
        4 * unit,
    )
    (d_gain,) = call(sum_kernel, "gain_sum", [shape((heads, width))], [term])
    whole = (tokens, heads, width)
    return (
        normed.reshape(whole),
        d_query.reshape(whole),
        d_key.reshape(whole),
        d_value.reshape(whole),
        d_state,
        d_gain,
    )


def solution(mesh):
    placed = (
        P("ctx", "tp", None),
        P("ctx", "tp", None),
        P("ctx", "tp", None),
        P("tp", None, None),
        P("tp", None),
        P("ctx", "tp", None),
    )
    return jax.shard_map(
        on_device,
        mesh=mesh,
        in_specs=placed,
        out_specs=(
            P("ctx", "tp", None),
            P("ctx", "tp", None),
            P("ctx", "tp", None),
            P("ctx", "tp", None),
            P("tp", None, None),
            P("tp", None),
        ),
        check_vma=False,
    )
```

```python
import functools

import jax
import jax.numpy as jnp
from jax import lax
from jax.experimental import pallas as pl
from jax.experimental.pallas import tpu as pltpu
from jax.sharding import PartitionSpec as P

F32 = jnp.float32
BF16 = jnp.bfloat16
EPS = 1e-06
NN = (((1,), (0,)), ((), ()))
NT = (((1,), (1,)), ((), ()))
TN = (((0,), (0,)), ((), ()))


def dot(a, b, dims):
    return lax.dot_general(a, b, dims, preferred_element_type=F32)


def split(a):
    high = a.astype(BF16)
    return high, (a - high.astype(F32)).astype(BF16)


def times(a, m, turned):
    high, low = split(m)
    both = jnp.concatenate([high, low], axis=1 if turned else 0)
    return dot(jnp.concatenate([a, a], axis=1), both, NT if turned else NN)


def head_rows(h, tokens, heads):
    return pl.ds(h, tokens, stride=heads)


def causal(tokens):
    rows = lax.broadcasted_iota(jnp.int32, (tokens, tokens), 0)
    cols = lax.broadcasted_iota(jnp.int32, (tokens, tokens), 1)
    return rows >= cols


def state_kernel(k_ref, v_ref, state_ref, kh_ref, vh_ref, k32, v32):
    heads, tokens, _ = kh_ref.shape
    k32[...] = k_ref[...].astype(F32)
    v32[...] = v_ref[...].astype(F32)
    for h in range(heads):
        k = k32[head_rows(h, tokens, heads), :].astype(BF16)
        v = v32[head_rows(h, tokens, heads), :].astype(BF16)
        state_ref[h] = dot(k, v, TN)
        kh_ref[h] = k
        vh_ref[h] = v


def local_kernel(q_ref, kh_ref, vh_ref, init_in, qh_ref, scores_ref, attn_ref, init_ref, q32):
    heads, tokens, _ = kh_ref.shape
    init_ref[...] = init_in[...]
    q32[...] = q_ref[...].astype(F32)
    keep = causal(tokens)
    for h in range(heads):
        q = q32[head_rows(h, tokens, heads), :].astype(BF16)
        qh_ref[h] = q
        scores = jnp.where(keep, dot(q, kh_ref[h], NT), 0.0).astype(BF16)
        scores_ref[h] = scores
        attn_ref[h] = dot(scores, vh_ref[h], NN)


def cot_kernel(c_ref, gain_ref, ch_ref, c32):
    heads, tokens, _ = ch_ref.shape
    c32[...] = c_ref[...].astype(F32)
    for h in range(heads):
        ch_ref[h] = c32[head_rows(h, tokens, heads), :]


def near_prefix_kernel(x_ref, pre_ref, total_ref):
    members, rows = x_ref.shape[:2]
    total = jnp.zeros(x_ref.shape[1:], F32)
    for i in range(members):
        pre_ref[i] = total
        total = total + x_ref[i]
    for g in range(total_ref.shape[0]):
        total_ref[g] = total


def far_prefix_kernel(totals_ref, pre_ref, out_ref):
    groups, (members, rows, width) = totals_ref.shape[0], pre_ref.shape
    own = lax.axis_index("ctx") // members
    far = jnp.zeros((rows, width), F32)
    for g in range(groups):
        far = far + jnp.where(g < own, totals_ref[g], 0.0)
    for i in range(members):
        out_ref[i] = far + pre_ref[i]


def near_suffix_kernel(x_ref, suf_ref, total_ref):
    members, rows = suf_ref.shape[:2]
    total = jnp.zeros(x_ref.shape[1:], F32)
    for i in reversed(range(members)):
        suf_ref[i] = total[:rows]
        total = total + x_ref[i]
    for g in range(total_ref.shape[0]):
        total_ref[g] = total


def far_suffix_kernel(totals_ref, suf_ref, out_ref, gain_ref):
    groups, (members, rows, width) = totals_ref.shape[0], suf_ref.shape
    own = lax.axis_index("ctx") // members
    far = jnp.zeros((rows, width), F32)
    total = jnp.zeros(totals_ref.shape[1:], F32)
    for g in range(groups):
        total = total + totals_ref[g]
        far = far + jnp.where(g > own, totals_ref[g, :rows], 0.0)
    for i in range(members):
        out_ref[i, :rows] = far + suf_ref[i]
        out_ref[i, rows:] = total[:rows]
    gain_ref[...] = total[rows : rows + gain_ref.shape[0]]


def attn_kernel(before_ref, init_ref, qh_ref, local_ref, ch_ref, gain_ref, attn_ref, state_ref, stats_ref):
    heads, tokens, width = qh_ref.shape
    ssq = jnp.zeros((tokens, width), F32)
    gdot = jnp.zeros((tokens, width), F32)
    for h in range(heads):
        state = init_ref[h] + before_ref[h]
        state_ref[h] = state
        attn = local_ref[h] + times(qh_ref[h], state, False)
        attn_ref[h] = attn
        ssq = ssq + attn * attn
        gdot = gdot + gain_ref[h : h + 1, :] * ch_ref[h] * attn
    ssq_row = jnp.sum(ssq.T, axis=0, keepdims=True)
    gdot_row = jnp.sum(gdot.T, axis=0, keepdims=True)
    half = tokens // 2
    rows = jnp.concatenate(
        [ssq_row[:, :half], ssq_row[:, half:], gdot_row[:, :half], gdot_row[:, half:]], axis=0
    )
    for i in range(stats_ref.shape[0]):
        stats_ref[i] = rows


def grad_kernel(width_total, stats_ref, attn_ref, ch_ref, gain_ref, qh_ref, dh_ref, grad_ref, scale_ref):
    heads, tokens, width = qh_ref.shape
    members, padded, _ = grad_ref.shape
    parts = members // heads
    chunk = width // parts
    rows = stats_ref[0]
    for i in range(1, stats_ref.shape[0]):
        rows = rows + stats_ref[i]
    ssq = jnp.concatenate([rows[0:1], rows[1:2]], axis=1)
    gdot = jnp.concatenate([rows[2:3], rows[3:4]], axis=1)
    rscale = lax.rsqrt(ssq / width_total + EPS)
    pull = rscale * rscale * rscale * gdot / width_total
    rscale = jnp.broadcast_to(rscale, (width, tokens)).T
    pull = jnp.broadcast_to(pull, (width, tokens)).T
    scale_ref[...] = rscale
    terms = []
    for h in range(heads):
        gain = gain_ref[h : h + 1, :]
        attn = attn_ref[h]
        pushed = ch_ref[h] * rscale
        d_attn = (gain * pushed - attn * pull).astype(BF16)
        dh_ref[h] = d_attn
        grad = dot(qh_ref[h], d_attn, TN)
        for p in range(parts):
            grad_ref[h * parts + p, :chunk] = grad[p * chunk : (p + 1) * chunk]
        terms.append(jnp.sum(pushed * attn, axis=0, keepdims=True))
    terms = jnp.concatenate(terms + [jnp.zeros((padded - chunk - heads, width), F32)], axis=0)
    for i in range(members):
        grad_ref[i, chunk:] = terms


def normed_kernel(attn_ref, gain_ref, scale_ref, normed_ref, out32):
    heads, tokens, _ = attn_ref.shape
    rscale = scale_ref[...]
    for h in range(heads):
        out32[head_rows(h, tokens, heads), :] = attn_ref[h] * rscale * gain_ref[h : h + 1, :]
    normed_ref[...] = out32[...].astype(BF16)


def back_kernel(dh_ref, vh_ref, kh_ref, qh_ref, state_ref, scores_ref, dq_ref, dk_ref, dv_ref, out32):
    heads, tokens, _ = kh_ref.shape
    keep = causal(tokens)
    for h in range(heads):
        d_attn = dh_ref[h]
        back = jnp.where(keep, dot(d_attn, vh_ref[h], NT), 0.0).astype(BF16)
        d_query = dot(back, kh_ref[h], NN) + times(d_attn, state_ref[h], True)
        out32[head_rows(h, tokens, heads), :] = d_query
        dk_ref[h] = dot(back, qh_ref[h], TN)
        dv_ref[h] = dot(scores_ref[h], d_attn, TN)
    dq_ref[...] = out32[...].astype(BF16)


def last_kernel(after_ref, kh_ref, vh_ref, dk_in, dv_in, dk_ref, dv_ref, d_state_ref, k32, v32):
    heads, tokens, width = kh_ref.shape
    parts = after_ref.shape[0] // heads
    chunk = width // parts
    for h in range(heads):
        pieces = [after_ref[h * parts + p, :chunk] for p in range(parts)]
        after = jnp.concatenate(pieces, axis=0)
        k32[head_rows(h, tokens, heads), :] = dk_in[h] + times(vh_ref[h], after, True)
        v32[head_rows(h, tokens, heads), :] = dv_in[h] + times(kh_ref[h], after, False)
        for p in range(parts):
            d_state_ref[h, p * chunk : (p + 1) * chunk] = after_ref[h * parts + p, chunk:]
    dk_ref[...] = k32[...].astype(BF16)
    dv_ref[...] = v32[...].astype(BF16)


def call(kernel, name, outs, args, scratch=(), flops=0):
    moved = sum(a.size * a.dtype.itemsize for a in list(args) + list(outs))
    return pl.pallas_call(
        kernel,
        name=name,
        out_shape=outs,
        in_specs=[pl.BlockSpec(memory_space=pltpu.VMEM)] * len(args),
        out_specs=[pl.BlockSpec(memory_space=pltpu.VMEM)] * len(outs),
        scratch_shapes=scratch,
        compiler_params=pltpu.CompilerParams(vmem_limit_bytes=24 * 2**20),
        cost_estimate=pl.CostEstimate(flops=flops, bytes_accessed=moved, transcendentals=0),
    )(*args)


def shape(dims, dtype=F32):
    return jax.ShapeDtypeStruct(dims, dtype)


def on_device(queries, keys, values, init_state, gain, cotangent):
    tokens, heads, width = queries.shape
    peers = lax.axis_size("ctx")
    sharers = lax.axis_size("tp")
    groups = 4
    members = peers // groups
    near = [[g * members + i for i in range(members)] for g in range(groups)]
    far = [[g * members + i for g in range(groups)] for i in range(members)]
    width_total = heads * sharers * width
    flat = (tokens * heads, width)
    by_head = (heads, tokens, width)
    states = (heads, width, width)
    chunk = heads * width // members
    chunks = (members, chunk, width)
    padded = chunk + 8
    squares = (heads, tokens, tokens)
    wide = pltpu.VMEM(flat, F32)
    unit = 2 * tokens * width * width * heads
    q, k, v, c = (a.reshape(flat) for a in (queries, keys, values, cotangent))

    def swap(x, lists):
        return lax.all_to_all(x, "ctx", 0, 0, axis_index_groups=lists)

    own, kh, vh = call(
        state_kernel,
        "state",
        [shape(states), shape(by_head, BF16), shape(by_head, BF16)],
        [k, v],
        [wide, wide],
        unit,
    )
    gathered = swap(own.reshape(chunks), near)
    qh, scores, local, init = call(
        local_kernel,
        "local",
        [shape(by_head, BF16), shape(squares, BF16), shape(by_head), shape(states)],
        [q, kh, vh, init_state],
        [wide],
        4 * unit,
    )
    pre, totals = call(
        near_prefix_kernel, "near_prefix", [shape(chunks), shape((groups, chunk, width))], [gathered]
    )
    totals = swap(totals, far)
    (ch,) = call(cot_kernel, "cotangent", [shape(by_head)], [c, gain], [wide])
    (before,) = call(far_prefix_kernel, "far_prefix", [shape(chunks)], [totals, pre])
    before = swap(before, near).reshape(states)
    attn, state, stats = call(
        attn_kernel,
        "attn",
        [shape(by_head), shape(states), shape((sharers, 4, tokens // 2))],
        [before, init, qh, local, ch, gain],
        (),
        2 * unit,
    )
    stats = lax.all_to_all(stats, "tp", 0, 0)
    dh, grad, scale = call(
        functools.partial(grad_kernel, width_total),
        "grad",
        [shape(by_head, BF16), shape((members, padded, width)), shape((tokens, width))],
        [stats, attn, ch, gain, qh],
        (),
        unit,
    )
    gathered = swap(grad, near)
    (normed,) = call(normed_kernel, "normed", [shape(flat, BF16)], [attn, gain, scale], [wide])
    suf, totals = call(
        near_suffix_kernel, "near_suffix", [shape(chunks), shape((groups, padded, width))], [gathered]
    )
    totals = swap(totals, far)
    d_query, dk, dv = call(
        back_kernel,
        "back",
        [shape(flat, BF16), shape(by_head), shape(by_head)],
        [dh, vh, kh, qh, state, scores],
        [wide],
        10 * unit,
    )
    after, d_gain = call(
        far_suffix_kernel,
        "far_suffix",
        [shape((members, 2 * chunk, width)), shape((heads, width))],
        [totals, suf],
    )
    after = swap(after, near)
    d_key, d_value, d_state = call(
        last_kernel,
        "last",
        [shape(flat, BF16), shape(flat, BF16), shape(states)],
        [after, kh, vh, dk, dv],
        [wide, wide],
        4 * unit,
    )
    whole = (tokens, heads, width)
    return (
        normed.reshape(whole),
        d_query.reshape(whole),
        d_key.reshape(whole),
        d_value.reshape(whole),
        d_state,
        d_gain,
    )


def solution(mesh):
    placed = (
        P("ctx", "tp", None),
        P("ctx", "tp", None),
        P("ctx", "tp", None),
        P("tp", None, None),
        P("tp", None),
        P("ctx", "tp", None),
    )
    return jax.shard_map(
        on_device,
        mesh=mesh,
        in_specs=placed,
        out_specs=(
            P("ctx", "tp", None),
            P("ctx", "tp", None),
            P("ctx", "tp", None),
            P("ctx", "tp", None),
            P("tp", None, None),
            P("tp", None),
        ),
        check_vma=False,
    )
```

```python
import functools

import jax
import jax.numpy as jnp
from jax import lax
from jax.experimental import pallas as pl
from jax.experimental.pallas import tpu as pltpu
from jax.sharding import PartitionSpec as P

F32 = jnp.float32
BF16 = jnp.bfloat16
EPS = 1e-06
NN = (((1,), (0,)), ((), ()))
NT = (((1,), (1,)), ((), ()))
TN = (((0,), (0,)), ((), ()))


def led_by(first, count):
    return (first,) + tuple(i for i in range(count) if i != first)


OUT1, BACK1 = led_by(10, 16), led_by(6, 16)
OUT2, BACK2 = led_by(6, 16), led_by(10, 16)
FAR1, FAR2 = (2, 0, 3, 1), (2, 0, 3, 1)


def found(out, back):
    return tuple(back.index(member) for member in out)


def dot(a, b, dims):
    return lax.dot_general(a, b, dims, preferred_element_type=F32)


def split(a):
    high = a.astype(BF16)
    return high, (a - high.astype(F32)).astype(BF16)


def times(a, m, turned):
    high, low = split(m)
    both = jnp.concatenate([high, low], axis=1 if turned else 0)
    return dot(jnp.concatenate([a, a], axis=1), both, NT if turned else NN)


def head_rows(h, tokens, heads):
    return pl.ds(h, tokens, stride=heads)


def causal(tokens):
    rows = lax.broadcasted_iota(jnp.int32, (tokens, tokens), 0)
    cols = lax.broadcasted_iota(jnp.int32, (tokens, tokens), 1)
    return rows >= cols


def state_kernel(k_hbm, v_hbm, state_ref, kh_ref, vh_ref, k_in, v_in, k32, v32, sems):
    heads, tokens, _ = kh_ref.shape
    k_copy = pltpu.make_async_copy(k_hbm, k_in, sems.at[0])
    v_copy = pltpu.make_async_copy(v_hbm, v_in, sems.at[1])
    k_copy.start()
    v_copy.start()
    k_copy.wait()
    k32[...] = k_in[...].astype(F32)
    v_copy.wait()
    v32[...] = v_in[...].astype(F32)
    for h in range(heads):
        k = k32[head_rows(h, tokens, heads), :].astype(BF16)
        v = v32[head_rows(h, tokens, heads), :].astype(BF16)
        state_ref[h] = dot(k, v, TN)
        kh_ref[h] = k
        vh_ref[h] = v


def local_kernel(
    q_ref, kh_ref, vh_ref, init_in, gain_in, qh_ref, scores_ref, attn_ref, init_ref, gain_ref, q32
):
    heads, tokens, _ = kh_ref.shape
    init_ref[...] = init_in[...]
    gain_ref[...] = gain_in[...]
    q32[...] = q_ref[...].astype(F32)
    keep = causal(tokens)
    for h in range(heads):
        q = q32[head_rows(h, tokens, heads), :].astype(BF16)
        qh_ref[h] = q
        scores = jnp.where(keep, dot(q, kh_ref[h], NT), 0.0).astype(BF16)
        scores_ref[h] = scores
        attn_ref[h] = dot(scores, vh_ref[h], NN)


def cot_kernel(c_ref, ch_ref, c32):
    heads, tokens, _ = ch_ref.shape
    c32[...] = c_ref[...].astype(F32)
    for h in range(heads):
        ch_ref[h] = c32[head_rows(h, tokens, heads), :].astype(BF16)


def near_prefix_kernel(x_ref, pre_ref, total_ref):
    members, rows = x_ref.shape[:2]
    total = jnp.zeros(x_ref.shape[1:], F32)
    for i in range(members):
        pre_ref[i] = total
        total = total + x_ref[OUT1.index(i)]
    for g in range(total_ref.shape[0]):
        total_ref[g] = total


def far_prefix_kernel(totals_ref, pre_ref, out_ref):
    groups, (members, rows, width) = totals_ref.shape[0], pre_ref.shape
    own = lax.axis_index("ctx") // members
    far = jnp.zeros((rows, width), F32)
    for g in range(groups):
        far = far + jnp.where(FAR1[g] < own, totals_ref[g], 0.0)
    for j in range(members):
        out_ref[j] = far + pre_ref[BACK1[j]]


def near_suffix_kernel(x_ref, suf_ref, total_ref):
    members, rows = suf_ref.shape[:2]
    total = jnp.zeros(x_ref.shape[1:], F32)
    for i in reversed(range(members)):
        suf_ref[i] = total[:rows]
        total = total + x_ref[OUT2.index(i)]
    for g in range(total_ref.shape[0]):
        total_ref[g] = total


def far_suffix_kernel(totals_ref, suf_ref, out_ref):
    groups, (members, rows, width) = totals_ref.shape[0], suf_ref.shape
    own = lax.axis_index("ctx") // members
    far = jnp.zeros((rows, width), F32)
    total = jnp.zeros((rows, width), F32)
    for g in range(groups):
        total = total + totals_ref[g, :rows]
        far = far + jnp.where(FAR2[g] > own, totals_ref[g, :rows], 0.0)
    for j in range(members):
        out_ref[j, :rows] = far + suf_ref[BACK2[j]]
        out_ref[j, rows:] = total


def attn_kernel(before_ref, init_ref, qh_ref, local_ref, ch_ref, gain_ref, attn_ref, state_ref, stats_ref):
    heads, tokens, width = qh_ref.shape
    parts = before_ref.shape[0] // heads
    places = found(OUT1, BACK1)
    ssq = jnp.zeros((tokens, width), F32)
    gdot = jnp.zeros((tokens, width), F32)
    for h in range(heads):
        pieces = [before_ref[j] for j in places[h * parts : (h + 1) * parts]]
        state = init_ref[h] + jnp.concatenate(pieces, axis=0)
        state_ref[h] = state
        attn = local_ref[h] + times(qh_ref[h], state, False)
        attn_ref[h] = attn
        ssq = ssq + attn * attn
        gdot = gdot + gain_ref[h : h + 1, :] * ch_ref[h].astype(F32) * attn
    ssq_row = jnp.sum(ssq.T, axis=0, keepdims=True)
    gdot_row = jnp.sum(gdot.T, axis=0, keepdims=True)
    half = tokens // 2
    rows = jnp.concatenate(
        [ssq_row[:, :half], ssq_row[:, half:], gdot_row[:, :half], gdot_row[:, half:]], axis=0
    )
    for i in range(stats_ref.shape[0]):
        stats_ref[i] = rows


def grad_kernel(width_total, stats_ref, attn_ref, ch_ref, gain_ref, qh_ref, dh_ref, grad_ref, scale_ref):
    heads, tokens, width = qh_ref.shape
    members, padded, _ = grad_ref.shape
    parts = members // heads
    chunk = width // parts
    rows = stats_ref[0]
    for i in range(1, stats_ref.shape[0]):
        rows = rows + stats_ref[i]
    ssq = jnp.concatenate([rows[0:1], rows[1:2]], axis=1)
    gdot = jnp.concatenate([rows[2:3], rows[3:4]], axis=1)
    rscale = lax.rsqrt(ssq / width_total + EPS)
    pull = rscale * rscale * rscale * gdot / width_total
    rscale = jnp.broadcast_to(rscale, (width, tokens)).T
    pull = jnp.broadcast_to(pull, (width, tokens)).T
    scale_ref[...] = rscale
    terms = []
    for h in range(heads):
        gain = gain_ref[h : h + 1, :]
        attn = attn_ref[h]
        pushed = ch_ref[h].astype(F32) * rscale
        d_attn = (gain * pushed - attn * pull).astype(BF16)
        dh_ref[h] = d_attn
        grad = dot(qh_ref[h], d_attn, TN)
        for p in range(parts):
            grad_ref[h * parts + p, :chunk] = grad[p * chunk : (p + 1) * chunk]
        terms.append(jnp.sum(pushed * attn, axis=0, keepdims=True))
    terms = jnp.concatenate(terms + [jnp.zeros((padded - chunk - heads, width), F32)], axis=0)
    for i in range(members):
        grad_ref[i, chunk:] = terms


def normed_kernel(attn_ref, gain_ref, scale_ref, normed_ref, out32):
    heads, tokens, _ = attn_ref.shape
    rscale = scale_ref[...]
    for h in range(heads):
        out32[head_rows(h, tokens, heads), :] = attn_ref[h] * rscale * gain_ref[h : h + 1, :]
    normed_ref[...] = out32[...].astype(BF16)


def back_kernel(dh_ref, vh_ref, kh_ref, qh_ref, state_ref, scores_ref, dq_ref, dk_ref, dv_ref, out32):
    heads, tokens, _ = kh_ref.shape
    keep = causal(tokens)
    for h in range(heads):
        d_attn = dh_ref[h]
        back = jnp.where(keep, dot(d_attn, vh_ref[h], NT), 0.0).astype(BF16)
        d_query = dot(back, kh_ref[h], NN) + times(d_attn, state_ref[h], True)
        out32[head_rows(h, tokens, heads), :] = d_query
        dk_ref[h] = dot(back, qh_ref[h], TN)
        dv_ref[h] = dot(scores_ref[h], d_attn, TN)
    dq_ref[...] = out32[...].astype(BF16)


def last_kernel(
    after_ref, totals_ref, kh_ref, vh_ref, dk_in, dv_in,
    dk_hbm, dv_hbm, state_hbm, gain_hbm, k32, v32, dk, dv, states, gain, sems,
):
    heads, tokens, width = kh_ref.shape
    parts = after_ref.shape[0] // heads
    chunk = width // parts
    places = found(OUT2, BACK2)
    for h in range(heads):
        for p in range(parts):
            states[h, p * chunk : (p + 1) * chunk] = after_ref[places[h * parts + p], chunk:]
    state_copy = pltpu.make_async_copy(states, state_hbm, sems.at[0])
    state_copy.start()
    total = totals_ref[0, chunk:]
    for g in range(1, totals_ref.shape[0]):
        total = total + totals_ref[g, chunk:]
    gain[...] = total[:heads]
    gain_copy = pltpu.make_async_copy(gain, gain_hbm, sems.at[3])
    gain_copy.start()
    afters = []
    for h in range(heads):
        pieces = [after_ref[j, :chunk] for j in places[h * parts : (h + 1) * parts]]
        after = jnp.concatenate(pieces, axis=0)
        afters.append(after)
        k32[head_rows(h, tokens, heads), :] = dk_in[h] + times(vh_ref[h], after, True)
    dk[...] = k32[...].astype(BF16)
    dk_copy = pltpu.make_async_copy(dk, dk_hbm, sems.at[1])
    dk_copy.start()
    for h in range(heads):
        v32[head_rows(h, tokens, heads), :] = dv_in[h] + times(kh_ref[h], afters[h], False)
    dv[...] = v32[...].astype(BF16)
    dv_copy = pltpu.make_async_copy(dv, dv_hbm, sems.at[2])
    dv_copy.start()
    state_copy.wait()
    gain_copy.wait()
    dk_copy.wait()
    dv_copy.wait()


def call(kernel, name, outs, args, scratch=(), flops=0, places=(pltpu.VMEM, pltpu.VMEM), limit=24):
    moved = sum(a.size * a.dtype.itemsize for a in list(args) + list(outs))
    return pl.pallas_call(
        kernel,
        name=name,
        out_shape=outs,
        in_specs=[pl.BlockSpec(memory_space=places[0])] * len(args),
        out_specs=[pl.BlockSpec(memory_space=places[1])] * len(outs),
        scratch_shapes=scratch,
        compiler_params=pltpu.CompilerParams(vmem_limit_bytes=limit * 2**20),
        cost_estimate=pl.CostEstimate(flops=flops, bytes_accessed=moved, transcendentals=0),
    )(*args)


def shape(dims, dtype=F32):
    return jax.ShapeDtypeStruct(dims, dtype)


def on_device(queries, keys, values, init_state, gain, cotangent):
    tokens, heads, width = queries.shape
    peers = lax.axis_size("ctx")
    sharers = lax.axis_size("tp")
    groups = 4
    members = peers // groups
    def near(order):
        return [[g * members + i for i in order] for g in range(groups)]

    def far(order):
        return [[g * members + i for g in order] for i in range(members)]

    width_total = heads * sharers * width
    flat = (tokens * heads, width)
    by_head = (heads, tokens, width)
    states = (heads, width, width)
    chunk = heads * width // members
    chunks = (members, chunk, width)
    padded = chunk + 8
    squares = (heads, tokens, tokens)
    wide = pltpu.VMEM(flat, F32)
    half = pltpu.VMEM(flat, BF16)
    unit = 2 * tokens * width * width * heads
    q, k, v, c = (a.reshape(flat) for a in (queries, keys, values, cotangent))

    def swap(x, lists):
        return lax.all_to_all(x, "ctx", 0, 0, axis_index_groups=lists)

    own, kh, vh = call(
        state_kernel,
        "state",
        [shape(states), shape(by_head, BF16), shape(by_head, BF16)],
        [pltpu.with_memory_space_constraint(k, pltpu.HBM), pltpu.with_memory_space_constraint(v, pltpu.HBM)],
        [half, half, wide, wide, pltpu.SemaphoreType.DMA((2,))],
        unit,
        (pltpu.HBM, pltpu.VMEM),
    )
    gathered = swap(own.reshape(chunks), near(OUT1))
    pre, totals = call(
        near_prefix_kernel, "near_prefix", [shape(chunks), shape((groups, chunk, width))], [gathered]
    )
    totals = swap(totals, far(FAR1))
    totals, q, c, init_state = lax.optimization_barrier((totals, q, c, init_state))
    qh, scores, local, init, gain = call(
        local_kernel,
        "local",
        [shape(by_head, BF16), shape(squares, BF16), shape(by_head), shape(states), shape((heads, width))],
        [q, kh, vh, init_state, gain],
        [wide],
        4 * unit,
    )
    (ch,) = call(cot_kernel, "cotangent", [shape(by_head, BF16)], [c], [wide])
    (before,) = call(far_prefix_kernel, "far_prefix", [shape(chunks)], [totals, pre])
    before = swap(before, near(BACK1))
    attn, state, stats = call(
        attn_kernel,
        "attn",
        [shape(by_head), shape(states), shape((sharers, 4, tokens // 2))],
        [before, init, qh, local, ch, gain],
        (),
        2 * unit,
    )
    stats = lax.all_to_all(stats, "tp", 0, 0)
    dh, grad, scale = call(
        functools.partial(grad_kernel, width_total),
        "grad",
        [shape(by_head, BF16), shape((members, padded, width)), shape((tokens, width))],
        [stats, attn, ch, gain, qh],
        (),
        unit,
    )
    gathered = swap(grad, near(OUT2))
    (normed,) = call(normed_kernel, "normed", [shape(flat, BF16)], [attn, gain, scale], [wide])
    suf, totals = call(
        near_suffix_kernel, "near_suffix", [shape(chunks), shape((groups, padded, width))], [gathered]
    )
    d_query, dk, dv = call(
        back_kernel,
        "back",
        [shape(flat, BF16), shape(by_head), shape(by_head)],
        [dh, vh, kh, qh, state, scores],
        [wide],
        10 * unit,
    )
    totals, normed, d_query, dk, dv = lax.optimization_barrier((totals, normed, d_query, dk, dv))
    totals = swap(totals, far(FAR2))
    (after,) = call(
        far_suffix_kernel, "far_suffix", [shape((members, 2 * chunk, width))], [totals, suf]
    )
    after = swap(after, near(BACK2))
    d_key, d_value, d_state, d_gain = call(
        last_kernel,
        "last",
        [shape(flat, BF16), shape(flat, BF16), shape(states), shape((heads, width))],
        [after, totals, kh, vh, dk, dv],
        [
            wide,
            wide,
            half,
            half,
            pltpu.VMEM(states, F32),
            pltpu.VMEM((heads, width), F32),
            pltpu.SemaphoreType.DMA((4,)),
        ],
        4 * unit,
        (pltpu.VMEM, pltpu.HBM),
    )
    whole = (tokens, heads, width)
    return (
        normed.reshape(whole),
        d_query.reshape(whole),
        d_key.reshape(whole),
        d_value.reshape(whole),
        d_state,
        d_gain,
    )


def solution(mesh):
    placed = (
        P("ctx", "tp", None),
        P("ctx", "tp", None),
        P("ctx", "tp", None),
        P("tp", None, None),
        P("tp", None),
        P("ctx", "tp", None),
    )
    return jax.shard_map(
        on_device,
        mesh=mesh,
        in_specs=placed,
        out_specs=(
            P("ctx", "tp", None),
            P("ctx", "tp", None),
            P("ctx", "tp", None),
            P("ctx", "tp", None),
            P("tp", None, None),
            P("tp", None),
        ),
        check_vma=False,
    )
```

```python
import functools

import jax
import jax.numpy as jnp
from jax import lax
from jax.experimental import pallas as pl
from jax.experimental.pallas import tpu as pltpu
from jax.sharding import PartitionSpec as P

F32 = jnp.float32
BF16 = jnp.bfloat16
EPS = 1e-06
NN = (((1,), (0,)), ((), ()))
NT = (((1,), (1,)), ((), ()))
TN = (((0,), (0,)), ((), ()))


def led_by(first, count):
    return [first] + [i for i in range(count) if i != first]


OUT1, BACK1 = led_by(10, 16), led_by(6, 16)
OUT2, BACK2 = led_by(6, 16), led_by(10, 16)
FAR1, FAR2 = [2, 0, 3, 1], [2, 0, 3, 1]


def found(out, back):
    return tuple(back.index(member) for member in out)


def dot(a, b, dims):
    return lax.dot_general(a, b, dims, preferred_element_type=F32)


def split(a):
    high = a.astype(BF16)
    return high, (a - high.astype(F32)).astype(BF16)


def times(a, parts, turned):
    both = jnp.concatenate(parts, axis=1 if turned else 0)
    return dot(jnp.concatenate([a, a], axis=1), both, NT if turned else NN)


def head_rows(h, tokens, heads):
    return pl.ds(h, tokens, stride=heads)


def masked(a, b, keep):
    return jnp.where(keep, dot(a, b, NT), 0.0).astype(BF16)


def causal(tokens):
    rows = lax.broadcasted_iota(jnp.int32, (tokens, tokens), 0)
    cols = lax.broadcasted_iota(jnp.int32, (tokens, tokens), 1)
    return rows >= cols


def state_kernel(k_hbm, v_hbm, state_ref, kh_ref, vh_ref, k_in, v_in, k32, v32, sems):
    heads, tokens, _ = kh_ref.shape
    k_copy = pltpu.make_async_copy(k_hbm, k_in, sems.at[0])
    v_copy = pltpu.make_async_copy(v_hbm, v_in, sems.at[1])
    k_copy.start()
    v_copy.start()
    k_copy.wait()
    k32[...] = k_in[...].astype(F32)
    v_copy.wait()
    v32[...] = v_in[...].astype(F32)
    for h in range(heads):
        k = k32[head_rows(h, tokens, heads), :].astype(BF16)
        v = v32[head_rows(h, tokens, heads), :].astype(BF16)
        state_ref[h] = dot(k, v, TN)
        kh_ref[h] = k
        vh_ref[h] = v


def local_kernel(
    q_ref, kh_ref, vh_ref, init_in, gain_in, qh_ref, attn_ref, init_ref, gain_ref, q32
):
    heads, tokens, _ = kh_ref.shape
    init_ref[...] = init_in[...]
    gain_ref[...] = gain_in[...]
    q32[...] = q_ref[...].astype(F32)
    keep = causal(tokens)
    for h in range(heads):
        q = q32[head_rows(h, tokens, heads), :].astype(BF16)
        qh_ref[h] = q
        attn_ref[h] = dot(masked(q, kh_ref[h], keep), vh_ref[h], NN)


def cot_kernel(c_ref, ch_ref, c32):
    heads, tokens, _ = ch_ref.shape
    c32[...] = c_ref[...].astype(F32)
    for h in range(heads):
        ch_ref[h] = c32[head_rows(h, tokens, heads), :].astype(BF16)


def near_prefix_kernel(x_ref, pre_ref, total_ref):
    members, rows = x_ref.shape[:2]
    total = jnp.zeros(x_ref.shape[1:], F32)
    for i in range(members):
        pre_ref[i] = total
        total = total + x_ref[OUT1.index(i)]
    for g in range(total_ref.shape[0]):
        total_ref[g] = total


def far_prefix_kernel(totals_ref, pre_ref, out_ref):
    groups, (members, rows, width) = totals_ref.shape[0], pre_ref.shape
    own = lax.axis_index("ctx") // members
    far = jnp.zeros((rows, width), F32)
    for g in range(groups):
        far = far + jnp.where(FAR1[g] < own, totals_ref[g], 0.0)
    for j in range(members):
        out_ref[j] = far + pre_ref[BACK1[j]]


def near_suffix_kernel(x_ref, suf_ref, total_ref):
    members, rows = suf_ref.shape[:2]
    total = jnp.zeros(x_ref.shape[1:], F32)
    for i in reversed(range(members)):
        suf_ref[i] = total[:rows]
        total = total + x_ref[OUT2.index(i)]
    for g in range(total_ref.shape[0]):
        total_ref[g] = total


def far_suffix_kernel(totals_ref, suf_ref, out_ref):
    groups, (members, rows, width) = totals_ref.shape[0], suf_ref.shape
    own = lax.axis_index("ctx") // members
    far = jnp.zeros((rows, width), F32)
    total = jnp.zeros((rows, width), F32)
    for g in range(groups):
        total = total + totals_ref[g, :rows]
        far = far + jnp.where(FAR2[g] > own, totals_ref[g, :rows], 0.0)
    for j in range(members):
        out_ref[j, :rows] = far + suf_ref[BACK2[j]]
        out_ref[j, rows:] = total


def attn_kernel(before_ref, init_ref, qh_ref, local_ref, ch_ref, gain_ref, attn_ref, state_ref, stats_ref):
    heads, tokens, width = qh_ref.shape
    parts = before_ref.shape[0] // heads
    places = found(OUT1, BACK1)
    ssq = jnp.zeros((tokens, width), F32)
    gdot = jnp.zeros((tokens, width), F32)
    for h in range(heads):
        pieces = [before_ref[j] for j in places[h * parts : (h + 1) * parts]]
        state = init_ref[h] + jnp.concatenate(pieces, axis=0)
        state_ref[h] = state
        attn = local_ref[h] + times(qh_ref[h], split(state), False)
        attn_ref[h] = attn
        ssq = ssq + attn * attn
        gdot = gdot + gain_ref[h : h + 1, :] * ch_ref[h].astype(F32) * attn
    ssq_row = jnp.sum(ssq.T, axis=0, keepdims=True)
    gdot_row = jnp.sum(gdot.T, axis=0, keepdims=True)
    half = tokens // 2
    rows = jnp.concatenate(
        [ssq_row[:, :half], ssq_row[:, half:], gdot_row[:, :half], gdot_row[:, half:]], axis=0
    )
    for i in range(stats_ref.shape[0]):
        stats_ref[i] = rows


def query_grad(dh_ref, kh_ref, vh_ref, state_ref, dq_ref, out32):
    heads, tokens, _ = kh_ref.shape
    keep = causal(tokens)
    for h in range(heads):
        d_attn = dh_ref[h]
        back = masked(d_attn, vh_ref[h], keep)
        d_query = dot(back, kh_ref[h], NN) + times(d_attn, split(state_ref[h]), True)
        out32[head_rows(h, tokens, heads), :] = d_query
    dq_ref[...] = out32[...].astype(BF16)


def down(row, width):
    return jnp.broadcast_to(row, (width, row.shape[1])).T


def normed_rows(attn_ref, gain_ref, scale_ref, normed_ref, out32):
    heads, tokens, width = attn_ref.shape
    rscale = down(scale_ref[...], width)
    for h in range(heads):
        out32[head_rows(h, tokens, heads), :] = attn_ref[h] * rscale * gain_ref[h : h + 1, :]
    normed_ref[...] = out32[...].astype(BF16)


def finished_rows(
    dh_ref, kh_ref, vh_ref, state_ref, attn_ref, gain_ref, scale_ref, dq_hbm, normed_hbm, dq, normed, wide, sems
):
    query_grad(dh_ref, kh_ref, vh_ref, state_ref, dq, wide)
    dq_copy = pltpu.make_async_copy(dq, dq_hbm, sems.at[0])
    dq_copy.start()
    normed_rows(attn_ref, gain_ref, scale_ref, normed, wide)
    normed_copy = pltpu.make_async_copy(normed, normed_hbm, sems.at[1])
    normed_copy.start()
    dq_copy.wait()
    normed_copy.wait()


def first_core():
    return lax.axis_index("tp") % 2 == 0


def grad_kernel(
    width_total, stats_ref, attn_ref, ch_ref, gain_ref, qh_ref, kh_ref, vh_ref, state_ref,
    dh_ref, grad_ref, scale_ref, dq_hbm, normed_hbm, dq, normed, wide, sems,
):
    heads, tokens, width = qh_ref.shape
    members, padded, _ = grad_ref.shape
    parts = members // heads
    chunk = width // parts
    rows = stats_ref[0]
    for i in range(1, stats_ref.shape[0]):
        rows = rows + stats_ref[i]
    ssq = jnp.concatenate([rows[0:1], rows[1:2]], axis=1)
    gdot = jnp.concatenate([rows[2:3], rows[3:4]], axis=1)
    rscale = lax.rsqrt(ssq / width_total + EPS)
    pull = rscale * rscale * rscale * gdot / width_total
    scale_ref[...] = rscale
    rscale = down(rscale, width)
    pull = down(pull, width)
    terms = []
    for h in range(heads):
        gain = gain_ref[h : h + 1, :]
        attn = attn_ref[h]
        pushed = ch_ref[h].astype(F32) * rscale
        d_attn = (gain * pushed - attn * pull).astype(BF16)
        dh_ref[h] = d_attn
        grad = dot(qh_ref[h], d_attn, TN)
        for p in range(parts):
            grad_ref[h * parts + p, :chunk] = grad[p * chunk : (p + 1) * chunk]
        terms.append(jnp.sum(pushed * attn, axis=0, keepdims=True))
    terms = jnp.concatenate(terms + [jnp.zeros((padded - chunk - heads, width), F32)], axis=0)
    for i in range(members):
        grad_ref[i, chunk:] = terms

    @pl.when(first_core())
    def _():
        finished_rows(
            dh_ref, kh_ref, vh_ref, state_ref, attn_ref, gain_ref, scale_ref,
            dq_hbm, normed_hbm, dq, normed, wide, sems,
        )


def back_kernel(
    dh_ref, vh_ref, kh_ref, qh_ref, state_ref, attn_ref, gain_ref, scale_ref, dq_in, normed_in,
    dq_hbm, normed_hbm, dk_ref, dv_ref, dq, normed, wide, sems,
):
    heads, tokens, _ = kh_ref.shape
    keep = causal(tokens)
    for h in range(heads):
        q, d_attn = qh_ref[h], dh_ref[h]
        dk_ref[h] = dot(masked(d_attn, vh_ref[h], keep), q, TN)
        dv_ref[h] = dot(masked(q, kh_ref[h], keep), d_attn, TN)

    @pl.when(jnp.logical_not(first_core()))
    def _():
        finished_rows(
            dh_ref, kh_ref, vh_ref, state_ref, attn_ref, gain_ref, scale_ref,
            dq_hbm, normed_hbm, dq, normed, wide, sems,
        )


def last_kernel(
    after_ref, totals_ref, kh_ref, vh_ref, dk_in, dv_in,
    dk_hbm, dv_hbm, state_hbm, gain_hbm, k32, v32, dk, dv, states, gain, sems,
):
    heads, tokens, width = kh_ref.shape
    parts = after_ref.shape[0] // heads
    chunk = width // parts
    places = found(OUT2, BACK2)
    for h in range(heads):
        for p in range(parts):
            states[h, p * chunk : (p + 1) * chunk] = after_ref[places[h * parts + p], chunk:]
    state_copy = pltpu.make_async_copy(states, state_hbm, sems.at[0])
    state_copy.start()
    total = totals_ref[0, chunk:]
    for g in range(1, totals_ref.shape[0]):
        total = total + totals_ref[g, chunk:]
    gain[...] = total[:heads]
    gain_copy = pltpu.make_async_copy(gain, gain_hbm, sems.at[3])
    gain_copy.start()
    afters = []
    for h in range(heads):
        pieces = [after_ref[j, :chunk] for j in places[h * parts : (h + 1) * parts]]
        after = split(jnp.concatenate(pieces, axis=0))
        afters.append(after)
        k32[head_rows(h, tokens, heads), :] = dk_in[h] + times(vh_ref[h], after, True)
    dk[...] = k32[...].astype(BF16)
    dk_copy = pltpu.make_async_copy(dk, dk_hbm, sems.at[1])
    dk_copy.start()
    for h in range(heads):
        v32[head_rows(h, tokens, heads), :] = dv_in[h] + times(kh_ref[h], afters[h], False)
    dv[...] = v32[...].astype(BF16)
    dv_copy = pltpu.make_async_copy(dv, dv_hbm, sems.at[2])
    dv_copy.start()
    state_copy.wait()
    gain_copy.wait()
    dk_copy.wait()
    dv_copy.wait()


def call(kernel, name, outs, args, scratch=(), flops=0, hbm_args=(), hbm_outs=(), aliases={}):
    moved = sum(a.size * a.dtype.itemsize for a in list(args) + list(outs))

    def places(count, hbm):
        return [pl.BlockSpec(memory_space=pltpu.HBM if i in hbm else pltpu.VMEM) for i in range(count)]

    return pl.pallas_call(
        kernel,
        name=name,
        out_shape=outs,
        in_specs=places(len(args), hbm_args),
        out_specs=places(len(outs), hbm_outs),
        scratch_shapes=scratch,
        input_output_aliases=aliases,
        compiler_params=pltpu.CompilerParams(vmem_limit_bytes=24 * 2**20),
        cost_estimate=pl.CostEstimate(flops=flops, bytes_accessed=moved, transcendentals=0),
    )(*args)


def shape(dims, dtype=F32):
    return jax.ShapeDtypeStruct(dims, dtype)


def on_device(queries, keys, values, init_state, gain, cotangent):
    tokens, heads, width = queries.shape
    peers = lax.axis_size("ctx")
    sharers = lax.axis_size("tp")
    groups = 4
    members = peers // groups
    def near(order):
        return [[g * members + i for i in order] for g in range(groups)]

    def far(order):
        return [[g * members + i for g in order] for i in range(members)]

    width_total = heads * sharers * width
    flat = (tokens * heads, width)
    by_head = (heads, tokens, width)
    states = (heads, width, width)
    chunk = heads * width // members
    chunks = (members, chunk, width)
    padded = chunk + 8
    wide = pltpu.VMEM(flat, F32)
    half = pltpu.VMEM(flat, BF16)
    unit = 2 * tokens * width * width * heads
    q, k, v, c = (a.reshape(flat) for a in (queries, keys, values, cotangent))

    def swap(x, lists):
        return lax.all_to_all(x, "ctx", 0, 0, axis_index_groups=lists)

    own, kh, vh = call(
        state_kernel,
        "state",
        [shape(states), shape(by_head, BF16), shape(by_head, BF16)],
        [pltpu.with_memory_space_constraint(a, pltpu.HBM) for a in (k, v)],
        [half, half, wide, wide, pltpu.SemaphoreType.DMA((2,))],
        unit,
        hbm_args=(0, 1),
    )
    gathered = swap(own.reshape(chunks), near(OUT1))
    pre, totals = call(
        near_prefix_kernel, "near_prefix", [shape(chunks), shape((groups, chunk, width))], [gathered]
    )
    totals = swap(totals, far(FAR1))
    totals, q, c, init_state = lax.optimization_barrier((totals, q, c, init_state))
    qh, local, init, gain = call(
        local_kernel,
        "local",
        [shape(by_head, BF16), shape(by_head), shape(states), shape((heads, width))],
        [q, kh, vh, init_state, gain],
        [wide],
        4 * unit,
    )
    (ch,) = call(cot_kernel, "cotangent", [shape(by_head, BF16)], [c], [wide])
    (before,) = call(far_prefix_kernel, "far_prefix", [shape(chunks)], [totals, pre])
    before = swap(before, near(BACK1))
    attn, state, stats = call(
        attn_kernel,
        "attn",
        [shape(by_head), shape(states), shape((sharers, 4, tokens // 2))],
        [before, init, qh, local, ch, gain],
        (),
        2 * unit,
    )
    stats = lax.all_to_all(stats, "tp", 0, 0, axis_index_groups=[led_by(5, sharers)])
    dh, grad, scale, d_query, normed = call(
        functools.partial(grad_kernel, width_total),
        "grad",
        [
            shape(by_head, BF16),
            shape((members, padded, width)),
            shape((1, tokens)),
            shape(flat, BF16),
            shape(flat, BF16),
        ],
        [stats, attn, ch, gain, qh, kh, vh, state],
        [half, half, wide, pltpu.SemaphoreType.DMA((2,))],
        5 * unit,
        hbm_outs=(3, 4),
    )
    gathered = swap(grad, near(OUT2))
    suf, totals = call(
        near_suffix_kernel, "near_suffix", [shape(chunks), shape((groups, padded, width))], [gathered]
    )
    d_query, normed, dk, dv = call(
        back_kernel,
        "back",
        [shape(flat, BF16), shape(flat, BF16), shape(by_head), shape(by_head)],
        [dh, vh, kh, qh, state, attn, gain, scale, d_query, normed],
        [half, half, wide, pltpu.SemaphoreType.DMA((2,))],
        10 * unit,
        hbm_args=(8, 9),
        hbm_outs=(0, 1),
        aliases={8: 0, 9: 1},
    )
    totals, normed, d_query, dk, dv = lax.optimization_barrier((totals, normed, d_query, dk, dv))
    totals = swap(totals, far(FAR2))
    (after,) = call(
        far_suffix_kernel, "far_suffix", [shape((members, 2 * chunk, width))], [totals, suf]
    )
    after = swap(after, near(BACK2))
    d_key, d_value, d_state, d_gain = call(
        last_kernel,
        "last",
        [shape(flat, BF16), shape(flat, BF16), shape(states), shape((heads, width))],
        [after, totals, kh, vh, dk, dv],
        [
            wide,
            wide,
            half,
            half,
            pltpu.VMEM(states, F32),
            pltpu.VMEM((heads, width), F32),
            pltpu.SemaphoreType.DMA((4,)),
        ],
        4 * unit,
        hbm_outs=(0, 1, 2, 3),
    )
    whole = (tokens, heads, width)
    return (
        normed.reshape(whole),
        d_query.reshape(whole),
        d_key.reshape(whole),
        d_value.reshape(whole),
        d_state,
        d_gain,
    )


def solution(mesh):
    placed = (
        P("ctx", "tp", None),
        P("ctx", "tp", None),
        P("ctx", "tp", None),
        P("tp", None, None),
        P("tp", None),
        P("ctx", "tp", None),
    )
    return jax.shard_map(
        on_device,
        mesh=mesh,
        in_specs=placed,
        out_specs=(
            P("ctx", "tp", None),
            P("ctx", "tp", None),
            P("ctx", "tp", None),
            P("ctx", "tp", None),
            P("tp", None, None),
            P("tp", None),
        ),
        check_vma=False,
    )
```

```python
import functools

import jax
import jax.numpy as jnp
from jax import lax
from jax.experimental import pallas as pl
from jax.experimental.pallas import tpu as pltpu
from jax.sharding import PartitionSpec as P

F32 = jnp.float32
BF16 = jnp.bfloat16
EPS = 1e-06
NN = (((1,), (0,)), ((), ()))
NT = (((1,), (1,)), ((), ()))
TN = (((0,), (0,)), ((), ()))


def led_by(first, count):
    return [first] + [i for i in range(count) if i != first]


OUT1, BACK1 = led_by(10, 16), led_by(6, 16)
OUT2, BACK2 = led_by(6, 16), led_by(10, 16)
FAR1, FAR2 = [2, 0, 3, 1], [2, 0, 3, 1]


def found(out, back):
    return tuple(back.index(member) for member in out)


def dot(a, b, dims):
    return lax.dot_general(a, b, dims, preferred_element_type=F32)


def split(a):
    high = a.astype(BF16)
    return high, (a - high.astype(F32)).astype(BF16)


def times(a, parts, turned):
    both = jnp.concatenate(parts, axis=1 if turned else 0)
    return dot(jnp.concatenate([a, a], axis=1), both, NT if turned else NN)


def head_rows(h, tokens, heads):
    return pl.ds(h, tokens, stride=heads)


def masked(a, b, keep):
    return jnp.where(keep, dot(a, b, NT), 0.0).astype(BF16)


def causal(tokens):
    rows = lax.broadcasted_iota(jnp.int32, (tokens, tokens), 0)
    cols = lax.broadcasted_iota(jnp.int32, (tokens, tokens), 1)
    return rows >= cols


def state_kernel(k_hbm, v_hbm, state_ref, kh_ref, vh_ref, k_in, v_in, k32, v32, sems):
    heads, tokens, _ = kh_ref.shape
    k_copy = pltpu.make_async_copy(k_hbm, k_in, sems.at[0])
    v_copy = pltpu.make_async_copy(v_hbm, v_in, sems.at[1])
    k_copy.start()
    v_copy.start()
    k_copy.wait()
    k32[...] = k_in[...].astype(F32)
    v_copy.wait()
    v32[...] = v_in[...].astype(F32)
    for h in range(heads):
        k = k32[head_rows(h, tokens, heads), :].astype(BF16)
        v = v32[head_rows(h, tokens, heads), :].astype(BF16)
        state_ref[h] = dot(k, v, TN)
        kh_ref[h] = k
        vh_ref[h] = v


def local_kernel(
    q_ref, kh_ref, vh_ref, init_in, gain_in, qh_ref, attn_ref, init_ref, gain_ref, q32
):
    heads, tokens, _ = kh_ref.shape
    init_ref[...] = init_in[...]
    gain_ref[...] = gain_in[...]
    q32[...] = q_ref[...].astype(F32)
    keep = causal(tokens)
    for h in range(heads):
        q = q32[head_rows(h, tokens, heads), :].astype(BF16)
        qh_ref[h] = q
        attn_ref[h] = dot(masked(q, kh_ref[h], keep), vh_ref[h], NN)


def cot_kernel(c_ref, ch_ref, c32):
    heads, tokens, _ = ch_ref.shape
    c32[...] = c_ref[...].astype(F32)
    for h in range(heads):
        ch_ref[h] = c32[head_rows(h, tokens, heads), :].astype(BF16)


def near_prefix_kernel(x_ref, pre_ref, total_ref):
    members, rows = x_ref.shape[:2]
    total = jnp.zeros(x_ref.shape[1:], F32)
    for i in range(members):
        pre_ref[i] = total
        total = total + x_ref[OUT1.index(i)]
    for g in range(total_ref.shape[0]):
        total_ref[g] = total


def far_prefix_kernel(totals_ref, pre_ref, out_ref):
    groups, (members, rows, width) = totals_ref.shape[0], pre_ref.shape
    own = lax.axis_index("ctx") // members
    far = jnp.zeros((rows, width), F32)
    for g in range(groups):
        far = far + jnp.where(FAR1[g] < own, totals_ref[g], 0.0)
    for j in range(members):
        out_ref[j] = far + pre_ref[BACK1[j]]


def near_suffix_kernel(x_ref, suf_ref, total_ref):
    members, rows, width = suf_ref.shape
    slot = x_ref.shape[0] // members
    total = jnp.zeros((rows, width), F32)
    terms = jnp.zeros((slot - rows, width), F32)
    for i in reversed(range(members)):
        first = OUT2.index(i) * slot
        suf_ref[i] = total
        total = total + x_ref[first : first + rows]
        terms = terms + x_ref[first + rows : first + slot]
    unused = jnp.zeros((total_ref.shape[1] - slot, width), F32)
    for g in range(total_ref.shape[0]):
        total_ref[g, :rows] = total
        total_ref[g, rows:] = jnp.concatenate([terms, unused], axis=0)


def far_suffix_kernel(totals_ref, suf_ref, out_ref):
    groups, (members, rows, width) = totals_ref.shape[0], suf_ref.shape
    own = lax.axis_index("ctx") // members
    far = jnp.zeros((rows, width), F32)
    total = jnp.zeros((rows, width), F32)
    for g in range(groups):
        total = total + totals_ref[g, :rows]
        far = far + jnp.where(FAR2[g] > own, totals_ref[g, :rows], 0.0)
    for j in range(members):
        out_ref[j, :rows] = far + suf_ref[BACK2[j]]
        out_ref[j, rows:] = total


def attn_kernel(before_ref, init_ref, qh_ref, local_ref, ch_ref, gain_ref, attn_ref, state_ref, stats_ref):
    heads, tokens, width = qh_ref.shape
    parts = before_ref.shape[0] // heads
    places = found(OUT1, BACK1)
    ssq = jnp.zeros((tokens, width), F32)
    gdot = jnp.zeros((tokens, width), F32)
    for h in range(heads):
        pieces = [before_ref[j] for j in places[h * parts : (h + 1) * parts]]
        state = init_ref[h] + jnp.concatenate(pieces, axis=0)
        state_ref[h] = state
        attn = local_ref[h] + times(qh_ref[h], split(state), False)
        attn_ref[h] = attn
        ssq = ssq + attn * attn
        gdot = gdot + gain_ref[h : h + 1, :] * ch_ref[h].astype(F32) * attn
    ssq_row = jnp.sum(ssq.T, axis=0, keepdims=True)
    gdot_row = jnp.sum(gdot.T, axis=0, keepdims=True)
    half = tokens // 2
    rows = jnp.concatenate(
        [ssq_row[:, :half], ssq_row[:, half:], gdot_row[:, :half], gdot_row[:, half:]], axis=0
    )
    for i in range(stats_ref.shape[0]):
        stats_ref[i] = rows


def query_grad(dh_ref, kh_ref, vh_ref, state_ref, dq_ref, out32):
    heads, tokens, _ = kh_ref.shape
    keep = causal(tokens)
    for h in range(heads):
        d_attn = dh_ref[h]
        back = masked(d_attn, vh_ref[h], keep)
        d_query = dot(back, kh_ref[h], NN) + times(d_attn, split(state_ref[h]), True)
        out32[head_rows(h, tokens, heads), :] = d_query
    dq_ref[...] = out32[...].astype(BF16)


def down(row, width):
    return jnp.broadcast_to(row, (width, row.shape[1])).T


def normed_rows(attn_ref, gain_ref, scale_ref, normed_ref, out32):
    heads, tokens, width = attn_ref.shape
    rscale = down(scale_ref[...], width)
    for h in range(heads):
        out32[head_rows(h, tokens, heads), :] = attn_ref[h] * rscale * gain_ref[h : h + 1, :]
    normed_ref[...] = out32[...].astype(BF16)


def finished_rows(
    dh_ref, kh_ref, vh_ref, state_ref, attn_ref, gain_ref, scale_ref, dq_hbm, normed_hbm, dq, normed, wide, sems
):
    query_grad(dh_ref, kh_ref, vh_ref, state_ref, dq, wide)
    dq_copy = pltpu.make_async_copy(dq, dq_hbm, sems.at[0])
    dq_copy.start()
    normed_rows(attn_ref, gain_ref, scale_ref, normed, wide)
    normed_copy = pltpu.make_async_copy(normed, normed_hbm, sems.at[1])
    normed_copy.start()
    dq_copy.wait()
    normed_copy.wait()


def first_core():
    return lax.axis_index("tp") % 2 == 0


def grad_kernel(
    width_total, stats_ref, attn_ref, ch_ref, gain_ref, qh_ref, kh_ref, vh_ref, state_ref,
    dh_ref, grad_ref, scale_ref, dq_hbm, normed_hbm, dq, normed, wide, sems,
):
    heads, tokens, width = qh_ref.shape
    parts = (grad_ref.shape[0] - heads * width) // (heads * heads)
    chunk = width // parts
    slot = chunk + heads
    rows = stats_ref[0]
    for i in range(1, stats_ref.shape[0]):
        rows = rows + stats_ref[i]
    ssq = jnp.concatenate([rows[0:1], rows[1:2]], axis=1)
    gdot = jnp.concatenate([rows[2:3], rows[3:4]], axis=1)
    rscale = lax.rsqrt(ssq / width_total + EPS)
    pull = rscale * rscale * rscale * gdot / width_total
    scale_ref[...] = rscale
    rscale = down(rscale, width)
    pull = down(pull, width)
    terms = []
    for h in range(heads):
        gain = gain_ref[h : h + 1, :]
        attn = attn_ref[h]
        pushed = ch_ref[h].astype(F32) * rscale
        d_attn = (gain * pushed - attn * pull).astype(BF16)
        dh_ref[h] = d_attn
        grad = dot(qh_ref[h], d_attn, TN)
        for p in range(parts):
            first = (h * parts + p) * slot
            grad_ref[first : first + chunk] = grad[p * chunk : (p + 1) * chunk]
        terms.append(jnp.sum(pushed * attn, axis=0, keepdims=True))
    terms = jnp.concatenate(terms, axis=0)
    for i in range(heads * parts):
        grad_ref[i * slot + chunk : (i + 1) * slot] = terms

    @pl.when(first_core())
    def _():
        finished_rows(
            dh_ref, kh_ref, vh_ref, state_ref, attn_ref, gain_ref, scale_ref,
            dq_hbm, normed_hbm, dq, normed, wide, sems,
        )


def back_kernel(
    dh_ref, vh_ref, kh_ref, qh_ref, state_ref, attn_ref, gain_ref, scale_ref, dq_in, normed_in,
    dq_hbm, normed_hbm, dk_ref, dv_ref, dq, normed, wide, sems,
):
    heads, tokens, _ = kh_ref.shape
    keep = causal(tokens)
    for h in range(heads):
        q, d_attn = qh_ref[h], dh_ref[h]
        dk_ref[h] = dot(masked(d_attn, vh_ref[h], keep), q, TN)
        dv_ref[h] = dot(masked(q, kh_ref[h], keep), d_attn, TN)

    @pl.when(jnp.logical_not(first_core()))
    def _():
        finished_rows(
            dh_ref, kh_ref, vh_ref, state_ref, attn_ref, gain_ref, scale_ref,
            dq_hbm, normed_hbm, dq, normed, wide, sems,
        )


def last_kernel(
    after_ref, totals_ref, kh_ref, vh_ref, dk_in, dv_in,
    dk_hbm, dv_hbm, state_hbm, gain_hbm, k32, v32, dk, dv, states, gain, sems,
):
    heads, tokens, width = kh_ref.shape
    parts = after_ref.shape[0] // heads
    chunk = width // parts
    places = found(OUT2, BACK2)
    for h in range(heads):
        for p in range(parts):
            states[h, p * chunk : (p + 1) * chunk] = after_ref[places[h * parts + p], chunk:]
    state_copy = pltpu.make_async_copy(states, state_hbm, sems.at[0])
    state_copy.start()
    total = totals_ref[0, chunk : chunk + heads]
    for g in range(1, totals_ref.shape[0]):
        total = total + totals_ref[g, chunk : chunk + heads]
    gain[...] = total
    gain_copy = pltpu.make_async_copy(gain, gain_hbm, sems.at[3])
    gain_copy.start()
    afters = []
    for h in range(heads):
        pieces = [after_ref[j, :chunk] for j in places[h * parts : (h + 1) * parts]]
        after = split(jnp.concatenate(pieces, axis=0))
        afters.append(after)
        k32[head_rows(h, tokens, heads), :] = dk_in[h] + times(vh_ref[h], after, True)
    dk[...] = k32[...].astype(BF16)
    dk_copy = pltpu.make_async_copy(dk, dk_hbm, sems.at[1])
    dk_copy.start()
    for h in range(heads):
        v32[head_rows(h, tokens, heads), :] = dv_in[h] + times(kh_ref[h], afters[h], False)
    dv[...] = v32[...].astype(BF16)
    dv_copy = pltpu.make_async_copy(dv, dv_hbm, sems.at[2])
    dv_copy.start()
    state_copy.wait()
    gain_copy.wait()
    dk_copy.wait()
    dv_copy.wait()


def call(kernel, name, outs, args, scratch=(), flops=0, hbm_args=(), hbm_outs=(), aliases={}):
    moved = sum(a.size * a.dtype.itemsize for a in list(args) + list(outs))

    def places(count, hbm):
        return [pl.BlockSpec(memory_space=pltpu.HBM if i in hbm else pltpu.VMEM) for i in range(count)]

    return pl.pallas_call(
        kernel,
        name=name,
        out_shape=outs,
        in_specs=places(len(args), hbm_args),
        out_specs=places(len(outs), hbm_outs),
        scratch_shapes=scratch,
        input_output_aliases=aliases,
        compiler_params=pltpu.CompilerParams(vmem_limit_bytes=24 * 2**20),
        cost_estimate=pl.CostEstimate(flops=flops, bytes_accessed=moved, transcendentals=0),
    )(*args)


def shape(dims, dtype=F32):
    return jax.ShapeDtypeStruct(dims, dtype)


def on_device(queries, keys, values, init_state, gain, cotangent):
    tokens, heads, width = queries.shape
    peers = lax.axis_size("ctx")
    sharers = lax.axis_size("tp")
    groups = 4
    members = peers // groups
    def near(order):
        return [[g * members + i for i in order] for g in range(groups)]

    def far(order):
        return [[g * members + i for g in order] for i in range(members)]

    width_total = heads * sharers * width
    flat = (tokens * heads, width)
    by_head = (heads, tokens, width)
    states = (heads, width, width)
    chunk = heads * width // members
    chunks = (members, chunk, width)
    padded = chunk + 8
    wide = pltpu.VMEM(flat, F32)
    half = pltpu.VMEM(flat, BF16)
    unit = 2 * tokens * width * width * heads
    q, k, v, c = (a.reshape(flat) for a in (queries, keys, values, cotangent))

    def swap(x, lists):
        return lax.all_to_all(x, "ctx", 0, 0, axis_index_groups=lists)

    own, kh, vh = call(
        state_kernel,
        "state",
        [shape(states), shape(by_head, BF16), shape(by_head, BF16)],
        [pltpu.with_memory_space_constraint(a, pltpu.HBM) for a in (k, v)],
        [half, half, wide, wide, pltpu.SemaphoreType.DMA((2,))],
        unit,
        hbm_args=(0, 1),
    )
    gathered = swap(own.reshape(chunks), near(OUT1))
    gathered, q, c, init_state = lax.optimization_barrier((gathered, q, c, init_state))
    pre, totals = call(
        near_prefix_kernel, "near_prefix", [shape(chunks), shape((groups, chunk, width))], [gathered]
    )
    totals = swap(totals, far(FAR1))
    qh, local, init, gain = call(
        local_kernel,
        "local",
        [shape(by_head, BF16), shape(by_head), shape(states), shape((heads, width))],
        [q, kh, vh, init_state, gain],
        [wide],
        4 * unit,
    )
    (ch,) = call(cot_kernel, "cotangent", [shape(by_head, BF16)], [c], [wide])
    totals, qh, local, init, gain, ch = lax.optimization_barrier(
        (totals, qh, local, init, gain, ch)
    )
    (before,) = call(far_prefix_kernel, "far_prefix", [shape(chunks)], [totals, pre])
    before = swap(before, near(BACK1))
    attn, state, stats = call(
        attn_kernel,
        "attn",
        [shape(by_head), shape(states), shape((sharers, 4, tokens // 2))],
        [before, init, qh, local, ch, gain],
        (),
        2 * unit,
    )
    stats = lax.all_to_all(stats, "tp", 0, 0, axis_index_groups=[led_by(5, sharers)])
    dh, grad, scale, d_query, normed = call(
        functools.partial(grad_kernel, width_total),
        "grad",
        [
            shape(by_head, BF16),
            shape((members * (chunk + heads), width)),
            shape((1, tokens)),
            shape(flat, BF16),
            shape(flat, BF16),
        ],
        [stats, attn, ch, gain, qh, kh, vh, state],
        [half, half, wide, pltpu.SemaphoreType.DMA((2,))],
        5 * unit,
        hbm_outs=(3, 4),
    )
    gathered = lax.all_to_all(
        grad.reshape(-1, heads, width), "ctx", 0, 0, axis_index_groups=near(OUT2), tiled=True
    ).reshape(grad.shape)
    suf, totals = call(
        near_suffix_kernel, "near_suffix", [shape(chunks), shape((groups, padded, width))], [gathered]
    )
    totals = swap(totals, far(FAR2))
    totals, dh = lax.optimization_barrier((totals, dh))
    (after,) = call(
        far_suffix_kernel, "far_suffix", [shape((members, 2 * chunk, width))], [totals, suf]
    )
    after = swap(after, near(BACK2))
    d_query, normed, dk, dv = call(
        back_kernel,
        "back",
        [shape(flat, BF16), shape(flat, BF16), shape(by_head), shape(by_head)],
        [dh, vh, kh, qh, state, attn, gain, scale, d_query, normed],
        [half, half, wide, pltpu.SemaphoreType.DMA((2,))],
        10 * unit,
        hbm_args=(8, 9),
        hbm_outs=(0, 1),
        aliases={8: 0, 9: 1},
    )
    d_key, d_value, d_state, d_gain = call(
        last_kernel,
        "last",
        [shape(flat, BF16), shape(flat, BF16), shape(states), shape((heads, width))],
        [after, totals, kh, vh, dk, dv],
        [
            wide,
            wide,
            half,
            half,
            pltpu.VMEM(states, F32),
            pltpu.VMEM((heads, width), F32),
            pltpu.SemaphoreType.DMA((4,)),
        ],
        4 * unit,
        hbm_outs=(0, 1, 2, 3),
    )
    whole = (tokens, heads, width)
    return (
        normed.reshape(whole),
        d_query.reshape(whole),
        d_key.reshape(whole),
        d_value.reshape(whole),
        d_state,
        d_gain,
    )


def solution(mesh):
    placed = (
        P("ctx", "tp", None),
        P("ctx", "tp", None),
        P("ctx", "tp", None),
        P("tp", None, None),
        P("tp", None),
        P("ctx", "tp", None),
    )
    return jax.shard_map(
        on_device,
        mesh=mesh,
        in_specs=placed,
        out_specs=(
            P("ctx", "tp", None),
            P("ctx", "tp", None),
            P("ctx", "tp", None),
            P("ctx", "tp", None),
            P("tp", None, None),
            P("tp", None),
        ),
        check_vma=False,
    )
```

```python
import functools

import jax
import jax.numpy as jnp
from jax import lax
from jax.experimental import pallas as pl
from jax.experimental.pallas import tpu as pltpu
from jax.sharding import PartitionSpec as P

F32 = jnp.float32
BF16 = jnp.bfloat16
EPS = 1e-06
NN = (((1,), (0,)), ((), ()))
NT = (((1,), (1,)), ((), ()))
TN = (((0,), (0,)), ((), ()))


def led_by(first, count):
    return [first] + [i for i in range(count) if i != first]


OUT1, BACK1 = led_by(10, 16), led_by(6, 16)
OUT2, BACK2 = led_by(6, 16), led_by(10, 16)
FAR1, FAR2 = [2, 0, 3, 1], [2, 0, 3, 1]


def found(out, back):
    return tuple(back.index(member) for member in out)


def dot(a, b, dims):
    return lax.dot_general(a, b, dims, preferred_element_type=F32)


def split(a):
    high = a.astype(BF16)
    return high, (a - high.astype(F32)).astype(BF16)


def times(a, parts, turned):
    both = jnp.concatenate(parts, axis=1 if turned else 0)
    return dot(jnp.concatenate([a, a], axis=1), both, NT if turned else NN)


def head_rows(h, tokens, heads):
    return pl.ds(h, tokens, stride=heads)


def masked(a, b, keep):
    return jnp.where(keep, dot(a, b, NT), 0.0).astype(BF16)


def causal(tokens):
    rows = lax.broadcasted_iota(jnp.int32, (tokens, tokens), 0)
    cols = lax.broadcasted_iota(jnp.int32, (tokens, tokens), 1)
    return rows >= cols


def state_kernel(k_hbm, v_hbm, state_ref, kh_ref, vh_ref, k_in, v_in, k32, v32, sems):
    heads, tokens, _ = kh_ref.shape
    k_copy = pltpu.make_async_copy(k_hbm, k_in, sems.at[0])
    v_copy = pltpu.make_async_copy(v_hbm, v_in, sems.at[1])
    k_copy.start()
    v_copy.start()
    k_copy.wait()
    k32[...] = k_in[...].astype(F32)
    v_copy.wait()
    v32[...] = v_in[...].astype(F32)
    for h in range(heads):
        k = k32[head_rows(h, tokens, heads), :].astype(BF16)
        v = v32[head_rows(h, tokens, heads), :].astype(BF16)
        state_ref[h] = dot(k, v, TN)
        kh_ref[h] = k
        vh_ref[h] = v


def local_kernel(
    q_ref, kh_ref, vh_ref, init_in, gain_in, qh_ref, attn_ref, init_ref, gain_ref, q32
):
    heads, tokens, _ = kh_ref.shape
    init_ref[...] = init_in[...]
    gain_ref[...] = gain_in[...]
    q32[...] = q_ref[...].astype(F32)
    keep = causal(tokens)
    for h in range(heads):
        q = q32[head_rows(h, tokens, heads), :].astype(BF16)
        qh_ref[h] = q
        attn_ref[h] = dot(masked(q, kh_ref[h], keep), vh_ref[h], NN)


def cot_kernel(c_ref, ch_ref, c32):
    heads, tokens, _ = ch_ref.shape
    c32[...] = c_ref[...].astype(F32)
    for h in range(heads):
        ch_ref[h] = c32[head_rows(h, tokens, heads), :].astype(BF16)


def near_prefix_kernel(x_ref, pre_ref, total_ref):
    members, rows = x_ref.shape[:2]
    total = jnp.zeros(x_ref.shape[1:], F32)
    for i in range(members):
        pre_ref[i] = total
        total = total + x_ref[OUT1.index(i)]
    for g in range(total_ref.shape[0]):
        total_ref[g] = total


def far_prefix_kernel(totals_ref, pre_ref, out_ref):
    groups, (members, rows, width) = totals_ref.shape[0], pre_ref.shape
    own = lax.axis_index("ctx") // members
    far = jnp.zeros((rows, width), F32)
    for g in range(groups):
        far = far + jnp.where(FAR1[g] < own, totals_ref[g], 0.0)
    for j in range(members):
        out_ref[j] = far + pre_ref[BACK1[j]]


def near_suffix_kernel(x_ref, suf_ref, total_ref):
    members, rows, width = suf_ref.shape
    slot = x_ref.shape[0] // members
    total = jnp.zeros((rows, width), F32)
    terms = jnp.zeros((slot - rows, width), F32)
    for i in reversed(range(members)):
        first = OUT2.index(i) * slot
        suf_ref[i] = total
        total = total + x_ref[first : first + rows]
        terms = terms + x_ref[first + rows : first + slot]
    unused = jnp.zeros((total_ref.shape[1] - slot, width), F32)
    for g in range(total_ref.shape[0]):
        total_ref[g, :rows] = total
        total_ref[g, rows:] = jnp.concatenate([terms, unused], axis=0)


def far_suffix_kernel(totals_ref, suf_ref, out_ref):
    groups, (members, rows, width) = totals_ref.shape[0], suf_ref.shape
    own = lax.axis_index("ctx") // members
    far = jnp.zeros((rows, width), F32)
    total = jnp.zeros((rows, width), F32)
    for g in range(groups):
        total = total + totals_ref[g, :rows]
        far = far + jnp.where(FAR2[g] > own, totals_ref[g, :rows], 0.0)
    for j in range(members):
        out_ref[j, :rows] = far + suf_ref[BACK2[j]]
        out_ref[j, rows:] = total


def attn_kernel(before_ref, init_ref, qh_ref, local_ref, ch_ref, gain_ref, attn_ref, state_ref, stats_ref):
    heads, tokens, width = qh_ref.shape
    parts = before_ref.shape[0] // heads
    places = found(OUT1, BACK1)
    ssq = jnp.zeros((tokens, width), F32)
    gdot = jnp.zeros((tokens, width), F32)
    for h in range(heads):
        pieces = [before_ref[j] for j in places[h * parts : (h + 1) * parts]]
        state = init_ref[h] + jnp.concatenate(pieces, axis=0)
        state_ref[h] = state
        attn = local_ref[h] + times(qh_ref[h], split(state), False)
        attn_ref[h] = attn
        ssq = ssq + attn * attn
        gdot = gdot + gain_ref[h : h + 1, :] * ch_ref[h].astype(F32) * attn
    ssq_row = jnp.sum(ssq.T, axis=0, keepdims=True)
    gdot_row = jnp.sum(gdot.T, axis=0, keepdims=True)
    half = tokens // 2
    rows = jnp.concatenate(
        [ssq_row[:, :half], ssq_row[:, half:], gdot_row[:, :half], gdot_row[:, half:]], axis=0
    )
    for i in range(stats_ref.shape[0]):
        stats_ref[i] = rows


def query_grad(dh_ref, kh_ref, vh_ref, state_ref, dq_ref, out32):
    heads, tokens, _ = kh_ref.shape
    keep = causal(tokens)
    for h in range(heads):
        d_attn = dh_ref[h]
        back = masked(d_attn, vh_ref[h], keep)
        d_query = dot(back, kh_ref[h], NN) + times(d_attn, split(state_ref[h]), True)
        out32[head_rows(h, tokens, heads), :] = d_query
    dq_ref[...] = out32[...].astype(BF16)


def down(row, width):
    return jnp.broadcast_to(row, (width, row.shape[1])).T


def normed_rows(attn_ref, gain_ref, scale_ref, normed_ref, out32):
    heads, tokens, width = attn_ref.shape
    rscale = down(scale_ref[...], width)
    for h in range(heads):
        out32[head_rows(h, tokens, heads), :] = attn_ref[h] * rscale * gain_ref[h : h + 1, :]
    normed_ref[...] = out32[...].astype(BF16)


def finished_rows(
    dh_ref, kh_ref, vh_ref, state_ref, attn_ref, gain_ref, scale_ref, dq_hbm, normed_hbm, dq, normed, wide, sems
):
    query_grad(dh_ref, kh_ref, vh_ref, state_ref, dq, wide)
    dq_copy = pltpu.make_async_copy(dq, dq_hbm, sems.at[0])
    dq_copy.start()
    normed_rows(attn_ref, gain_ref, scale_ref, normed, wide)
    normed_copy = pltpu.make_async_copy(normed, normed_hbm, sems.at[1])
    normed_copy.start()
    dq_copy.wait()
    normed_copy.wait()


def first_core():
    return lax.axis_index("tp") % 2 == 0


def grad_kernel(
    width_total, stats_ref, attn_ref, ch_ref, gain_ref, qh_ref, kh_ref, vh_ref, state_ref,
    dh_ref, grad_ref, scale_ref, dq_hbm, normed_hbm, dq, normed, wide, sems,
):
    heads, tokens, width = qh_ref.shape
    parts = (grad_ref.shape[0] - heads * width) // (heads * heads)
    chunk = width // parts
    slot = chunk + heads
    rows = stats_ref[0]
    for i in range(1, stats_ref.shape[0]):
        rows = rows + stats_ref[i]
    ssq = jnp.concatenate([rows[0:1], rows[1:2]], axis=1)
    gdot = jnp.concatenate([rows[2:3], rows[3:4]], axis=1)
    rscale = lax.rsqrt(ssq / width_total + EPS)
    pull = rscale * rscale * rscale * gdot / width_total
    scale_ref[...] = rscale
    rscale = down(rscale, width)
    pull = down(pull, width)
    terms = []
    for h in range(heads):
        gain = gain_ref[h : h + 1, :]
        attn = attn_ref[h]
        pushed = ch_ref[h].astype(F32) * rscale
        d_attn = (gain * pushed - attn * pull).astype(BF16)
        dh_ref[h] = d_attn
        grad = dot(qh_ref[h], d_attn, TN)
        for p in range(parts):
            first = (h * parts + p) * slot
            grad_ref[first : first + chunk] = grad[p * chunk : (p + 1) * chunk]
        terms.append(jnp.sum(pushed * attn, axis=0, keepdims=True))
    terms = jnp.concatenate(terms, axis=0)
    for i in range(heads * parts):
        grad_ref[i * slot + chunk : (i + 1) * slot] = terms

    @pl.when(first_core())
    def _():
        finished_rows(
            dh_ref, kh_ref, vh_ref, state_ref, attn_ref, gain_ref, scale_ref,
            dq_hbm, normed_hbm, dq, normed, wide, sems,
        )


def back_kernel(
    dh_ref, vh_ref, kh_ref, qh_ref, state_ref, attn_ref, gain_ref, scale_ref, dq_in, normed_in,
    dq_hbm, normed_hbm, dk_ref, dv_ref, dq, normed, wide, sems,
):
    heads, tokens, _ = kh_ref.shape
    keep = causal(tokens)
    for h in range(heads):
        q, d_attn = qh_ref[h], dh_ref[h]
        dk_ref[h] = dot(masked(d_attn, vh_ref[h], keep), q, TN)
        dv_ref[h] = dot(masked(q, kh_ref[h], keep), d_attn, TN)

    @pl.when(jnp.logical_not(first_core()))
    def _():
        finished_rows(
            dh_ref, kh_ref, vh_ref, state_ref, attn_ref, gain_ref, scale_ref,
            dq_hbm, normed_hbm, dq, normed, wide, sems,
        )


def last_kernel(
    after_ref, totals_ref, kh_ref, vh_ref, dk_in, dv_in,
    dk_hbm, dv_hbm, state_hbm, gain_hbm, k32, v32, dk, dv, states, gain, sems,
):
    heads, tokens, width = kh_ref.shape
    parts = after_ref.shape[0] // heads
    chunk = width // parts
    places = found(OUT2, BACK2)
    for h in range(heads):
        for p in range(parts):
            states[h, p * chunk : (p + 1) * chunk] = after_ref[places[h * parts + p], chunk:]
    state_copy = pltpu.make_async_copy(states, state_hbm, sems.at[0])
    state_copy.start()
    total = totals_ref[0, chunk : chunk + heads]
    for g in range(1, totals_ref.shape[0]):
        total = total + totals_ref[g, chunk : chunk + heads]
    gain[...] = total
    gain_copy = pltpu.make_async_copy(gain, gain_hbm, sems.at[3])
    gain_copy.start()
    afters = []
    for h in range(heads):
        pieces = [after_ref[j, :chunk] for j in places[h * parts : (h + 1) * parts]]
        after = split(jnp.concatenate(pieces, axis=0))
        afters.append(after)
        k32[head_rows(h, tokens, heads), :] = dk_in[h] + times(vh_ref[h], after, True)
    dk[...] = k32[...].astype(BF16)
    dk_copy = pltpu.make_async_copy(dk, dk_hbm, sems.at[1])
    dk_copy.start()
    for h in range(heads):
        v32[head_rows(h, tokens, heads), :] = dv_in[h] + times(kh_ref[h], afters[h], False)
    dv[...] = v32[...].astype(BF16)
    dv_copy = pltpu.make_async_copy(dv, dv_hbm, sems.at[2])
    dv_copy.start()
    state_copy.wait()
    gain_copy.wait()
    dk_copy.wait()
    dv_copy.wait()


def call(kernel, name, outs, args, scratch=(), flops=0, hbm_args=(), hbm_outs=(), aliases={}):
    moved = sum(a.size * a.dtype.itemsize for a in list(args) + list(outs))

    def places(count, hbm):
        return [pl.BlockSpec(memory_space=pltpu.HBM if i in hbm else pltpu.VMEM) for i in range(count)]

    return pl.pallas_call(
        kernel,
        name=name,
        out_shape=outs,
        in_specs=places(len(args), hbm_args),
        out_specs=places(len(outs), hbm_outs),
        scratch_shapes=scratch,
        input_output_aliases=aliases,
        compiler_params=pltpu.CompilerParams(vmem_limit_bytes=24 * 2**20),
        cost_estimate=pl.CostEstimate(flops=flops, bytes_accessed=moved, transcendentals=0),
    )(*args)


def shape(dims, dtype=F32):
    return jax.ShapeDtypeStruct(dims, dtype)


def on_device(queries, keys, values, init_state, gain, cotangent):
    tokens, heads, width = queries.shape
    peers = lax.axis_size("ctx")
    sharers = lax.axis_size("tp")
    groups = 4
    members = peers // groups
    def near(order):
        return [[g * members + i for i in order] for g in range(groups)]

    def far(order):
        return [[g * members + i for g in order] for i in range(members)]

    width_total = heads * sharers * width
    flat = (tokens * heads, width)
    by_head = (heads, tokens, width)
    states = (heads, width, width)
    chunk = heads * width // members
    chunks = (members, chunk, width)
    padded = chunk + 8
    wide = pltpu.VMEM(flat, F32)
    half = pltpu.VMEM(flat, BF16)
    unit = 2 * tokens * width * width * heads
    q, k, v, c = (a.reshape(flat) for a in (queries, keys, values, cotangent))

    def swap(x, lists):
        return lax.all_to_all(x, "ctx", 0, 0, axis_index_groups=lists)

    own, kh, vh = call(
        state_kernel,
        "state",
        [shape(states), shape(by_head, BF16), shape(by_head, BF16)],
        [pltpu.with_memory_space_constraint(a, pltpu.HBM) for a in (k, v)],
        [half, half, wide, wide, pltpu.SemaphoreType.DMA((2,))],
        unit,
        hbm_args=(0, 1),
    )
    gathered = swap(own.reshape(chunks), near(OUT1))
    gathered, q, c, init_state = lax.optimization_barrier((gathered, q, c, init_state))
    pre, totals = call(
        near_prefix_kernel, "near_prefix", [shape(chunks), shape((groups, chunk, width))], [gathered]
    )
    totals = swap(totals, far(FAR1))
    qh, local, init, gain = call(
        local_kernel,
        "local",
        [shape(by_head, BF16), shape(by_head), shape(states), shape((heads, width))],
        [q, kh, vh, init_state, gain],
        [wide],
        4 * unit,
    )
    (ch,) = call(cot_kernel, "cotangent", [shape(by_head, BF16)], [c], [wide])
    totals, qh, local, init, gain, ch = lax.optimization_barrier(
        (totals, qh, local, init, gain, ch)
    )
    (before,) = call(far_prefix_kernel, "far_prefix", [shape(chunks)], [totals, pre])
    before = swap(before, near(BACK1))
    attn, state, stats = call(
        attn_kernel,
        "attn",
        [shape(by_head), shape(states), shape((sharers, 4, tokens // 2))],
        [before, init, qh, local, ch, gain],
        (),
        2 * unit,
    )
    stats = lax.all_to_all(stats, "tp", 0, 0, axis_index_groups=[led_by(5, sharers)])
    dh, grad, scale, d_query, normed = call(
        functools.partial(grad_kernel, width_total),
        "grad",
        [
            shape(by_head, BF16),
            shape((members * (chunk + heads), width)),
            shape((1, tokens)),
            shape(flat, BF16),
            shape(flat, BF16),
        ],
        [stats, attn, ch, gain, qh, kh, vh, state],
        [half, half, wide, pltpu.SemaphoreType.DMA((2,))],
        5 * unit,
        hbm_outs=(3, 4),
    )
    gathered = lax.all_to_all(
        grad.reshape(-1, heads, width), "ctx", 0, 0, axis_index_groups=near(OUT2), tiled=True
    ).reshape(grad.shape)
    suf, totals = call(
        near_suffix_kernel, "near_suffix", [shape(chunks), shape((groups, padded, width))], [gathered]
    )
    d_query, normed, dk, dv = call(
        back_kernel,
        "back",
        [shape(flat, BF16), shape(flat, BF16), shape(by_head), shape(by_head)],
        [dh, vh, kh, qh, state, attn, gain, scale, d_query, normed],
        [half, half, wide, pltpu.SemaphoreType.DMA((2,))],
        10 * unit,
        hbm_args=(8, 9),
        hbm_outs=(0, 1),
        aliases={8: 0, 9: 1},
    )
    totals, normed, d_query, dk, dv = lax.optimization_barrier((totals, normed, d_query, dk, dv))
    totals = swap(totals, far(FAR2))
    (after,) = call(
        far_suffix_kernel, "far_suffix", [shape((members, 2 * chunk, width))], [totals, suf]
    )
    after = swap(after, near(BACK2))
    d_key, d_value, d_state, d_gain = call(
        last_kernel,
        "last",
        [shape(flat, BF16), shape(flat, BF16), shape(states), shape((heads, width))],
        [after, totals, kh, vh, dk, dv],
        [
            wide,
            wide,
            half,
            half,
            pltpu.VMEM(states, F32),
            pltpu.VMEM((heads, width), F32),
            pltpu.SemaphoreType.DMA((4,)),
        ],
        4 * unit,
        hbm_outs=(0, 1, 2, 3),
    )
    whole = (tokens, heads, width)
    return (
        normed.reshape(whole),
        d_query.reshape(whole),
        d_key.reshape(whole),
        d_value.reshape(whole),
        d_state,
        d_gain,
    )


def solution(mesh):
    placed = (
        P("ctx", "tp", None),
        P("ctx", "tp", None),
        P("ctx", "tp", None),
        P("tp", None, None),
        P("tp", None),
        P("ctx", "tp", None),
    )
    return jax.shard_map(
        on_device,
        mesh=mesh,
        in_specs=placed,
        out_specs=(
            P("ctx", "tp", None),
            P("ctx", "tp", None),
            P("ctx", "tp", None),
            P("ctx", "tp", None),
            P("tp", None, None),
            P("tp", None),
        ),
        check_vma=False,
    )
```
